256 devices in a mesh: ctx: 32 (over y, x, core), head: 8 (over z).
Axes of the slice: x: 4, y: 4, z: 8, core: 2. Of those that a mesh axis runs over, the one named last changes fastest.
Arguments:
- queries: bfloat16 [4096, 128, 576], P('ctx', 'head'), may hold values from -6 to 6
- out_grads: bfloat16 [4096, 128, 512], P('ctx', 'head'), may hold values from -6 to 6
- latent: bfloat16 [16384, 576], P('ctx'), may hold values from -6 to 6
- block_lists: int32 [64, 16], P('ctx'), may hold values from 0 to 255, as said below
- block_home: int32 [256], replicated, may hold values from 0 to 255, as said below
Outputs:
- query_grads: bfloat16 [4096, 128, 576], P('ctx', 'head')
- latent_grads: float32 [16384, 576], P('ctx')
The draws below stay inside these ranges and needn't reach their ends.
Inputs may be any that keep to these rules, and one draw needn't show every extreme that they name: Block b is stored at rows block_home[b]*64 to block_home[b]*64 + 63 of latent; block_home is a permutation. `block_lists`: each row names distinct blocks. Among the 32 entries of the rows of one index of ctx, at most 2 name blocks whose block_home lies in one range o*8 to o*8 + 7, and some range is named exactly 2 times.
All inputs are finite; a program needn't handle non-finite values.
Results may differ from the reference program's by a relative error of at most 0.0058.
Values may be sent and summed in bfloat16 or wider, within the bound.
No kernel may reach another device: no remote copies, remote signals or barrier semaphores. Data moves between devices by JAX's collectives and lax.ppermute only.
A program may use at most 128 MiB of HBM per device.

```python
import jax
import jax.numpy as jnp
from jax import lax

DC = 512
BLK = 64
QGRP = 64
TOPB = 16
KB_DEV = 8
LAT = 576
HEADS = 128
GROUPS = 2
CAP = 2
QTOK = 4096
NBLK = 256
KVTOK = 16384
N_CTX = 32


def placement_order(key):
    return jax.random.permutation(jax.random.fold_in(key, 303), NBLK).astype(jnp.int32)


def draw_queries(key, part):
    key = jax.random.fold_in(key, 2)
    base = jax.random.normal(key, (QTOK, HEADS, LAT), jnp.float32)
    return jnp.clip(base, -6.0, 6.0).astype(jnp.bfloat16)


def draw_latent(key, part):
    key = jax.random.fold_in(key, 1)
    base = jax.random.normal(key, (KVTOK, LAT), jnp.float32)
    return jnp.clip(base, -6.0, 6.0).astype(jnp.bfloat16)


def slab_entries(key, order):
    items = N_CTX * CAP
    mixed = jax.random.permutation(jax.random.fold_in(key, 11), items).astype(jnp.int32)
    hottest = mixed[0] // CAP
    item_ids = jnp.arange(items, dtype=jnp.int32)
    position = jnp.argsort(mixed).astype(jnp.int32)
    ranking = jnp.where(item_ids // CAP == hottest, item_ids - items, position)
    ordered = jnp.argsort(ranking).astype(jnp.int32)[:GROUPS * TOPB]
    shuffled = ordered[jax.random.permutation(jax.random.fold_in(key, 12), GROUPS * TOPB)]
    owners_of = shuffled // CAP
    copies = shuffled % CAP
    offsets = jax.random.randint(jax.random.fold_in(key, 13), (N_CTX,), 0, KB_DEV).astype(jnp.int32)
    within = (offsets[owners_of] + copies) % KB_DEV
    return order[owners_of * KB_DEV + within].reshape(GROUPS, TOPB)


def draw_block_lists(key, part):
    order = placement_order(key)
    key = jax.random.fold_in(key, 4)

    def one_slab(index):
        return slab_entries(jax.random.fold_in(key, index), order)
    slabs = jax.vmap(one_slab)(jnp.arange(N_CTX))
    return slabs.reshape(N_CTX * GROUPS, TOPB).astype(jnp.int32)


def draw_block_home(key, part):
    order = placement_order(key)
    return jnp.argsort(order).astype(jnp.int32)


def block_scale(stream_key, extent, cuts, smallest, top_value):
    def one(axis_at, blocks):
        heights = jax.random.uniform(jax.random.fold_in(jax.random.fold_in(stream_key, 6), axis_at), (blocks,), jnp.float32, smallest / len(cuts), top_value / len(cuts))
        return jnp.repeat(jnp.exp(heights), extent[axis_at] // blocks).reshape((-1,) + (1,) * (len(extent) - axis_at - 1))

    gain = one(*cuts[0])
    for cut in cuts[1:]:
        gain = gain * one(*cut)
    return gain


def gaussian(key, dims, spread, bound, cuts=(), kind=jnp.bfloat16):
    result = jax.random.normal(key, dims, jnp.float32) * spread
    if len(cuts) > 0:
        result = block_scale(key, dims, cuts, -0.22, 0.18) * result
    return jnp.clip(result, min=-bound, max=bound).astype(kind)


def setup_inputs(seed: int = 0) -> dict:
    key_of = jax.random.split(jax.random.key(seed), 6)
    return {
        "queries": draw_queries(jax.random.fold_in(key_of[5], 71), 0),
        "out_grads": gaussian(key_of[1], (QTOK, HEADS, DC), 1.0, 6.0, ((0, 32), (1, 8))),
        "latent": draw_latent(jax.random.fold_in(key_of[5], 71), 0),
        "block_lists": draw_block_lists(jax.random.fold_in(key_of[5], 71), 0),
        "block_home": draw_block_home(jax.random.fold_in(key_of[5], 71), 0),
    }


softmax_scale = 192.0 ** -0.5


def group_grads(query_rows, grad_rows, key_rows, value_width):
    query_full = query_rows.astype(jnp.float32)
    grad_full = grad_rows.astype(jnp.float32)
    key_full = key_rows.astype(jnp.float32)
    value_full = key_full[:, :value_width]
    scores = jnp.einsum("qhd,kd->qhk", query_full, key_full) * softmax_scale
    row_max = jnp.max(scores, axis=-1, keepdims=True)
    raised = jnp.exp(scores - row_max)
    weights = raised / jnp.sum(raised, axis=-1, keepdims=True)
    weights_half = lax.optimization_barrier(weights.astype(jnp.bfloat16)).astype(jnp.float32)
    attended = jnp.einsum("qhk,ke->qhe", weights_half, value_full)
    row_delta = jnp.sum(grad_full * attended, axis=-1, keepdims=True)
    weight_grad = jnp.einsum("qhe,ke->qhk", grad_full, value_full)
    score_grad = weights * (weight_grad - row_delta)
    score_half = lax.optimization_barrier(score_grad.astype(jnp.bfloat16)).astype(jnp.float32)
    query_part = (jnp.einsum("qhk,kd->qhd", score_half, key_full) * softmax_scale).astype(jnp.bfloat16)
    key_grad = jnp.einsum("qhk,qhd->kd", score_half, query_full) * softmax_scale
    value_grad = jnp.einsum("qhk,qhe->ke", weights_half, grad_full)
    key_grad = jnp.concatenate([key_grad[:, :value_width] + value_grad, key_grad[:, value_width:]], axis=1)
    return query_part, key_grad


def reference(queries, out_grads, latent, block_lists, block_home):
    value_width = out_grads.shape[-1]
    offsets = jnp.arange(BLK, dtype=jnp.int32)

    def one_group(running, index):
        start = (index * QGRP).astype(jnp.int32)
        query_rows = lax.dynamic_slice_in_dim(queries, start, QGRP, 0)
        grad_rows = lax.dynamic_slice_in_dim(out_grads, start, QGRP, 0)
        chosen = jnp.take(block_lists, index, axis=0)
        stored = jnp.take(block_home, chosen, axis=0).astype(jnp.int32)
        token_rows = (stored[:, None] * BLK + offsets[None, :]).reshape(-1)
        key_rows = jnp.take(latent, token_rows, axis=0)
        query_part, key_grad = group_grads(query_rows, grad_rows, key_rows, value_width)
        running = running.at[token_rows].add(key_grad)
        return running, query_part

    start_grads = jnp.zeros((KVTOK, LAT), jnp.float32)
    latent_grads, parts = lax.scan(one_group, start_grads, jnp.arange(N_CTX * GROUPS, dtype=jnp.int32))
    return parts.reshape(QTOK, HEADS, LAT).astype(jnp.bfloat16), latent_grads
```

```python
import functools

import jax
import jax.numpy as jnp
from jax import lax
from jax.experimental import pallas as pl
from jax.experimental.pallas import tpu as pltpu
from jax.sharding import PartitionSpec as P

BLK = 64
CHUNK = 256
LOG2E = 1.4426950408889634
softmax_scale = 192.0 ** (-0.5)
VMEM_LIMIT = 48 * 1024 * 1024


def plan_kernel(capacity, stored_blocks, lists_ref, home_ref, slot_ref, request_ref, entry_ref):
    groups, chosen = lists_ref.shape
    slots = request_ref.shape[0]

    def clear(s, carry):
        request_ref[s] = -1
        entry_ref[s] = 0
        return carry

    lax.fori_loop(0, slots, clear, 0, unroll=True)
    for group in range(groups):
        for at in range(chosen):
            entry = group * chosen + at
            stored = home_ref[lists_ref[group, at]]
            base = (stored // stored_blocks) * capacity
            slot = base + jnp.where(request_ref[base] >= 0, 1, 0)
            slot_ref[entry] = slot
            request_ref[slot] = stored % stored_blocks
            entry_ref[slot] = entry


def plan(block_lists, block_home, ctx_count, capacity, stored_blocks):
    entries = block_lists.shape[0] * block_lists.shape[1]
    slots = ctx_count * capacity
    smem = pl.BlockSpec(memory_space=pltpu.SMEM)
    return pl.pallas_call(
        functools.partial(plan_kernel, capacity, stored_blocks),
        out_shape=(
            jax.ShapeDtypeStruct((entries,), jnp.int32),
            jax.ShapeDtypeStruct((slots,), jnp.int32),
            jax.ShapeDtypeStruct((slots,), jnp.int32),
        ),
        in_specs=[smem, smem],
        out_specs=(smem, smem, smem),
        name="plan",
    )(block_lists, block_home)


def take_kernel(index_ref, rows_ref, out_ref):
    for at in range(out_ref.shape[0]):
        out_ref[at] = rows_ref[jnp.maximum(index_ref[at], 0)]


def take(index, rows):
    return pl.pallas_call(
        take_kernel,
        out_shape=jax.ShapeDtypeStruct((index.shape[0],) + rows.shape[1:], rows.dtype),
        in_specs=[pl.BlockSpec(memory_space=pltpu.SMEM), pl.BlockSpec(memory_space=pltpu.VMEM)],
        out_specs=pl.BlockSpec(memory_space=pltpu.VMEM),
        name="take",
    )(index, rows)


def gather_sum_kernel(index_ref, rows_ref, out_ref, total):
    total[...] = jnp.zeros_like(total)
    stored = out_ref.shape[0]
    for at in range(rows_ref.shape[0]):
        index = index_ref[at]
        index = jnp.where(index < 0, stored, index)
        total[index] += rows_ref[at].astype(jnp.float32)
    out_ref[...] = total[:stored]


def gather_sum(index, rows, stored):
    return pl.pallas_call(
        gather_sum_kernel,
        out_shape=jax.ShapeDtypeStruct((stored,) + rows.shape[1:], jnp.float32),
        in_specs=[pl.BlockSpec(memory_space=pltpu.SMEM), pl.BlockSpec(memory_space=pltpu.VMEM)],
        out_specs=pl.BlockSpec(memory_space=pltpu.VMEM),
        scratch_shapes=[pltpu.VMEM((stored + 1,) + rows.shape[1:], jnp.float32)],
        name="gather_sum",
    )(index, rows)


def group_kernel(value_width, *refs):
    key_refs = refs[:8]
    query_cols, query_rows, grad_cols, grad_rows = refs[8:12]
    query_out = refs[12]
    part_refs = refs[13:22]
    keys, keys_t, sums = refs[22:]
    step = pl.program_id(0)
    part = key_refs[0].shape[-2]

    @pl.when(step == 0)
    def _():
        for at in range(8):
            rows = key_refs[at][...].reshape(part, keys.shape[1])
            keys[at * part : (at + 1) * part, :] = rows
            keys_t[:, at * part : (at + 1) * part] = rows.T
        sums[...] = jnp.zeros_like(sums)

    scores = jnp.dot(keys[...], query_cols[...], preferred_element_type=jnp.float32)
    factor = softmax_scale * LOG2E
    top = jnp.max(scores, axis=0, keepdims=True)
    raised = jnp.exp2((scores - top) * factor)
    weights = raised * (1.0 / jnp.sum(raised, axis=0, keepdims=True))
    half = weights.astype(jnp.bfloat16)
    weight_grad = jnp.dot(
        keys[:, :value_width], grad_cols[...], preferred_element_type=jnp.float32
    )
    delta = jnp.sum(half.astype(jnp.float32) * weight_grad, axis=0, keepdims=True)
    score_half = (weights * (weight_grad - delta)).astype(jnp.bfloat16)
    query_out[...] = (
        jnp.dot(keys_t[...], score_half, preferred_element_type=jnp.float32) * softmax_scale
    ).astype(jnp.bfloat16)
    from_scores = (
        jnp.dot(score_half, query_rows[...], preferred_element_type=jnp.float32) * softmax_scale
    )
    from_values = jnp.dot(half, grad_rows[...], preferred_element_type=jnp.float32)
    sums[:, :value_width] += from_scores[:, :value_width] + from_values
    sums[:, value_width:] += from_scores[:, value_width:]

    @pl.when(step == pl.num_programs(0) - 1)
    def _():
        for at in range(7):
            part_refs[at][...] = sums[at * part : (at + 1) * part, :].astype(part_refs[at].dtype)
        middle = 7 * part + part // 2
        part_refs[7][...] = sums[7 * part : middle, :].astype(jnp.bfloat16)
        part_refs[8][...] = sums[middle:, :].astype(jnp.bfloat16)


def group_grads(group, key_parts, query_cols, query_rows, grad_cols, grad_rows):
    part, width = key_parts[0].shape[-2:]
    rows = query_cols.shape[-1]
    value_width = grad_rows.shape[-1]
    key_count = 8 * part
    steps = rows // CHUNK
    key_specs = []
    for piece in key_parts:
        if piece.ndim == 3:
            key_specs.append(pl.BlockSpec((None, part, width), lambda i: (group, 0, 0)))
        else:
            key_specs.append(pl.BlockSpec((part, width), lambda i: (0, 0)))
    col_spec = lambda depth: pl.BlockSpec((None, depth, CHUNK), lambda i: (group, 0, i))
    row_spec = lambda wide: pl.BlockSpec((None, CHUNK, wide), lambda i: (group, i, 0))
    whole = lambda count: pl.BlockSpec((count, width), lambda i: (0, 0))
    out_shape = [jax.ShapeDtypeStruct((width, rows), jnp.bfloat16)]
    out_specs = [pl.BlockSpec((width, CHUNK), lambda i: (0, i))]
    for at in range(9):
        count = part if at < 7 else part // 2
        out_shape.append(
            jax.ShapeDtypeStruct((count, width), jnp.float32 if at == 0 else jnp.bfloat16)
        )
        out_specs.append(whole(count))
    flops = 2 * rows * key_count * (3 * width + 2 * value_width)
    return pl.pallas_call(
        functools.partial(group_kernel, value_width),
        grid=(steps,),
        in_specs=key_specs
        + [col_spec(width), row_spec(width), col_spec(value_width), row_spec(value_width)],
        out_specs=out_specs,
        out_shape=out_shape,
        scratch_shapes=[
            pltpu.VMEM((key_count, width), jnp.bfloat16),
            pltpu.VMEM((width, key_count), jnp.bfloat16),
            pltpu.VMEM((key_count, width), jnp.float32),
        ],
        compiler_params=pltpu.CompilerParams(vmem_limit_bytes=VMEM_LIMIT),
        cost_estimate=pl.CostEstimate(
            flops=flops, bytes_accessed=10_000_000, transcendentals=rows * key_count
        ),
        name="group_grads",
    )(*key_parts, query_cols, query_rows, grad_cols, grad_rows)


def shift(x, by):
    count = lax.axis_size("head")
    return lax.ppermute(x, "head", [(i, (i + by) % count) for i in range(count)])


def ring_gather(x, first_half, second_half):
    right, left = [x], [x]
    for _ in range(3):
        right.append(shift(right[-1], 1))
        left.append(shift(left[-1], -1))
    far_first = shift(first_half(right[3]), 1)
    far_second = shift(second_half(left[3]), -1)
    return right, left, far_first, far_second


def ring_scatter(parts):
    own, plus1, minus1, plus2, minus2, plus3, minus3, far_first, far_second = parts
    wide = jnp.float32

    def add(a, b):
        return (a.astype(wide) + b.astype(wide)).astype(jnp.bfloat16)

    count = far_first.shape[0]
    right = shift(far_first, 1)
    left = shift(far_second, -1)
    right = jnp.concatenate([add(plus3[:count], right), plus3[count:]], axis=0)
    left = jnp.concatenate([minus3[:count], add(minus3[count:], left)], axis=0)
    right, left = shift(right, 1), shift(left, -1)
    right, left = shift(add(plus2, right), 1), shift(add(minus2, left), -1)
    right, left = shift(add(plus1, right), 1), shift(add(minus1, left), -1)
    return (own + right.astype(wide) + left.astype(wide)).astype(jnp.bfloat16)


def local(queries, out_grads, latent, block_lists, block_home):
    ctx_count = lax.axis_size("ctx")
    head_count = lax.axis_size("head")
    me = lax.axis_index("head")
    groups, chosen = block_lists.shape
    tokens, heads, width = queries.shape
    value_width = out_grads.shape[2]
    group_rows = tokens // groups
    stored_blocks = latent.shape[0] // BLK
    entries = groups * chosen
    capacity = 2
    share = BLK // head_count

    slot_of, requests, entry_of = plan(
        block_lists, block_home, ctx_count, capacity, stored_blocks
    )
    requests_in = lax.all_to_all(
        requests.reshape(ctx_count, 1, capacity), "ctx", split_axis=0, concat_axis=0, tiled=True
    ).reshape(ctx_count * capacity)

    mine = lax.dynamic_slice_in_dim(
        latent.reshape(stored_blocks, BLK, width), me * share, share, 1
    )
    outgoing = take(requests_in, mine)
    arrived = lax.all_to_all(outgoing, "ctx", split_axis=0, concat_axis=0, tiled=True)
    picked = take(slot_of, arrived).reshape(groups, chosen * share, width)

    query_parts = queries.reshape(groups, group_rows, heads, width)
    grad_parts = out_grads.reshape(groups, group_rows, heads, value_width)
    rows = heads * group_rows
    query_cols = query_parts.transpose(0, 3, 2, 1).reshape(groups, width, rows)
    query_rows = query_parts.transpose(0, 2, 1, 3).reshape(groups, rows, width)
    grad_cols = grad_parts.transpose(0, 3, 2, 1).reshape(groups, value_width, rows)
    grad_rows = grad_parts.transpose(0, 2, 1, 3).reshape(groups, rows, value_width)

    right, left, far_first, far_second = ring_gather(picked, lambda x: x[0], lambda x: x[1])
    near = [picked, left[1], right[1], left[2], right[2], left[3], right[3]]
    query_outs, sums = [], []
    for group in range(groups):
        far = far_first if group == 0 else far_second
        outs = group_grads(group, near + [far], query_cols, query_rows, grad_cols, grad_rows)
        query_outs.append(outs[0])
        sums.append(ring_scatter(outs[1:]))
    query_grads = jnp.stack(query_outs).reshape(groups, width, heads, group_rows)
    query_grads = query_grads.transpose(0, 3, 2, 1).reshape(tokens, heads, width)

    summed = jnp.concatenate(sums, axis=0).reshape(entries, share, width)
    returned = lax.all_to_all(
        take(entry_of, summed), "ctx", split_axis=0, concat_axis=0, tiled=True
    )
    total = gather_sum(requests_in, returned, stored_blocks)

    right, left, far_first, far_second = ring_gather(
        total, lambda x: x[: stored_blocks // 2], lambda x: x[stored_blocks // 2 :]
    )
    far = jnp.concatenate([far_first, far_second], axis=0)
    by_offset = [total, left[1], left[2], left[3], far, right[3], right[2], right[1]]
    pieces = jnp.stack(by_offset, axis=1)
    pieces = jnp.roll(pieces, me, axis=1)
    latent_grads = pieces.reshape(stored_blocks * BLK, width)
    return query_grads, latent_grads


def solution(mesh):
    in_specs = (P("ctx", "head", None), P("ctx", "head", None), P("ctx", None), P("ctx", None), P())
    out_specs = (P("ctx", "head", None), P("ctx", None))
    return jax.shard_map(local, mesh=mesh, in_specs=in_specs, out_specs=out_specs, check_vma=False)
```

```python
import functools

import jax
import jax.numpy as jnp
from jax import lax
from jax.experimental import pallas as pl
from jax.experimental.pallas import tpu as pltpu
from jax.sharding import PartitionSpec as P

BLK = 64
CAPACITY = 2
QUARTERS = 4
LOG2E = 1.4426950408889634
softmax_scale = 192.0 ** (-0.5)
VMEM_LIMIT = 56 * 1024 * 1024
ROWS_BY_ROWS = (((1,), (1,)), ((), ()))
COLS_BY_COLS = (((0,), (0,)), ((), ()))


def smem():
    return pl.BlockSpec(memory_space=pltpu.SMEM)


def vmem():
    return pl.BlockSpec(memory_space=pltpu.VMEM)


def plan_kernel(stored_blocks, lists_ref, home_ref, slot_ref, request_ref, entry_ref):
    groups, chosen = lists_ref.shape
    owners = request_ref.shape[0]
    for owner in range(owners):
        for copy in range(CAPACITY):
            request_ref[owner, 0, copy] = -1
            entry_ref[owner * CAPACITY + copy] = 0
    for group in range(groups):
        for at in range(chosen):
            entry = group * chosen + at
            stored = home_ref[lists_ref[group, at]]
            owner = stored // stored_blocks
            copy = jnp.where(request_ref[owner, 0, 0] >= 0, 1, 0)
            slot = owner * CAPACITY + copy
            slot_ref[entry] = slot
            request_ref[owner, 0, copy] = stored % stored_blocks
            entry_ref[slot] = entry


def plan(block_lists, block_home, ctx_count, stored_blocks):
    entries = block_lists.shape[0] * block_lists.shape[1]
    return pl.pallas_call(
        functools.partial(plan_kernel, stored_blocks),
        out_shape=(
            jax.ShapeDtypeStruct((entries,), jnp.int32),
            jax.ShapeDtypeStruct((ctx_count, 1, CAPACITY), jnp.int32),
            jax.ShapeDtypeStruct((ctx_count * CAPACITY,), jnp.int32),
        ),
        in_specs=[smem(), smem()],
        out_specs=(smem(), smem(), smem()),
        name="plan",
    )(block_lists, block_home)


def read_index(index_ref, at):
    if len(index_ref.shape) == 3:
        return index_ref[at // CAPACITY, 0, at % CAPACITY]
    return index_ref[at]


def take_kernel(index_ref, rows_ref, out_ref):
    for at in range(out_ref.shape[0]):
        out_ref[at] = rows_ref[jnp.maximum(read_index(index_ref, at), 0)]


def take(index, rows):
    return pl.pallas_call(
        take_kernel,
        out_shape=jax.ShapeDtypeStruct((index.size,) + rows.shape[1:], rows.dtype),
        in_specs=[smem(), vmem()],
        out_specs=vmem(),
        name="take",
    )(index, rows)


def pick_kernel(index_ref, rows_ref, out_ref):
    groups, subs, chosen = out_ref.shape[:3]
    for group in range(groups):
        for at in range(chosen):
            slot = index_ref[group * chosen + at]
            for sub in range(subs):
                out_ref[group, sub, at] = rows_ref[slot, sub]


def pick(index, rows, groups):
    chosen = index.shape[0] // groups
    shape = (groups, rows.shape[1], chosen) + rows.shape[2:]
    return pl.pallas_call(
        pick_kernel,
        out_shape=jax.ShapeDtypeStruct(shape, rows.dtype),
        in_specs=[smem(), vmem()],
        out_specs=vmem(),
        name="pick",
    )(index, rows)


def gather_sum_kernel(index_ref, rows_ref, out_ref, total):
    total[...] = jnp.zeros_like(total)
    stored = out_ref.shape[0]
    for at in range(rows_ref.shape[0]):
        index = read_index(index_ref, at)
        index = jnp.where(index < 0, stored, index)
        total[index] += rows_ref[at].astype(jnp.float32)
    out_ref[...] = total[:stored].astype(out_ref.dtype)


def gather_sum(index, rows, stored):
    return pl.pallas_call(
        gather_sum_kernel,
        out_shape=jax.ShapeDtypeStruct((stored,) + rows.shape[1:], jnp.bfloat16),
        in_specs=[smem(), vmem()],
        out_specs=vmem(),
        scratch_shapes=[pltpu.VMEM((stored + 1,) + rows.shape[1:], jnp.float32)],
        name="gather_sum",
    )(index, rows)


OFFSETS = ((0, 4), (1, -3), (-1, 3), (2, -2))


def group_kernel(value_width, me_ref, own_ref, *refs):
    key_refs = refs[:6]
    query_ref, grad_ref = refs[6:8]
    query_out = refs[8]
    part_refs = refs[9:17]
    keys, sums = refs[17:]
    step = pl.program_id(0)
    part = own_ref.shape[0]

    keys[:part, :] = own_ref[...]
    for group in range(2):

        @pl.when(step == group)
        def _():
            for at in range(3):
                keys[(at + 1) * part : (at + 2) * part, :] = key_refs[group * 3 + at][...]

    scores = lax.dot_general(
        keys[...], query_ref[...], ROWS_BY_ROWS, preferred_element_type=jnp.float32
    )
    factor = softmax_scale * LOG2E
    top = jnp.max(scores, axis=0, keepdims=True) * factor
    raised = jnp.exp2(scores * factor - top)
    weights = raised * (1.0 / jnp.sum(raised, axis=0, keepdims=True))
    half = weights.astype(jnp.bfloat16)
    weight_grad = lax.dot_general(
        keys[:, :value_width], grad_ref[...], ROWS_BY_ROWS, preferred_element_type=jnp.float32
    )
    delta = jnp.sum(half.astype(jnp.float32) * weight_grad, axis=0, keepdims=True)
    score_half = (weights * (weight_grad - delta)).astype(jnp.bfloat16)
    from_scores = (
        jnp.dot(score_half, query_ref[...], preferred_element_type=jnp.float32) * softmax_scale
    )
    from_values = jnp.dot(half, grad_ref[...], preferred_element_type=jnp.float32)
    sums[:, :value_width] = from_scores[:, :value_width] + from_values
    sums[:, value_width:] = from_scores[:, value_width:]
    query_out[...] = (
        lax.dot_general(
            keys[...], score_half, COLS_BY_COLS, preferred_element_type=jnp.float32
        )
        * softmax_scale
    ).astype(jnp.bfloat16)

    me = me_ref[0]
    half_part = part // 2
    for at in range(4):
        sub = ((me + OFFSETS[at][0] + 8) % 8) // 4
        for which in range(2):
            use = sub if which == 0 else 1 - sub
            start = pl.multiple_of(at * part + use * half_part, half_part)
            out = part_refs[at * 2 + which]
            out[...] = sums[pl.ds(start, half_part), :].astype(out.dtype)


def group_grads(me, own, key_parts, query_rows, grad_rows):
    groups, part, width = own.shape
    rows, value_width = grad_rows.shape[1:]
    key_count = QUARTERS * part
    by_group = lambda *shape: pl.BlockSpec((None,) + shape, lambda i: (i, 0, 0))
    whole = lambda *shape: pl.BlockSpec(shape, lambda i: (0, 0))
    out_shape = [jax.ShapeDtypeStruct((groups, width, rows), jnp.bfloat16)]
    out_specs = [by_group(width, rows)]
    for at in range(8):
        kind = jnp.float32 if at == 0 else jnp.bfloat16
        out_shape.append(jax.ShapeDtypeStruct((groups, part // 2, width), kind))
        out_specs.append(by_group(part // 2, width))
    flops = 2 * groups * rows * key_count * (3 * width + 2 * value_width)
    return pl.pallas_call(
        functools.partial(group_kernel, value_width),
        grid=(groups,),
        in_specs=[smem(), by_group(part, width)]
        + [whole(part, width)] * 6
        + [by_group(rows, width), by_group(rows, value_width)],
        out_specs=out_specs,
        out_shape=out_shape,
        scratch_shapes=[
            pltpu.VMEM((key_count, width), jnp.bfloat16),
            pltpu.VMEM((key_count, width), jnp.float32),
        ],
        compiler_params=pltpu.CompilerParams(vmem_limit_bytes=VMEM_LIMIT),
        cost_estimate=pl.CostEstimate(
            flops=flops, bytes_accessed=15_000_000, transcendentals=groups * rows * key_count
        ),
        name="group_grads",
    )(me, own, *key_parts, query_rows, grad_rows)


def shift(x, by):
    count = lax.axis_size("head")
    return lax.ppermute(x, "head", [(i, (i + by) % count) for i in range(count)])


def add(a, b):
    return (a.astype(jnp.float32) + b.astype(jnp.float32)).astype(jnp.bfloat16)


def ring_scatter(parts, group):
    if group == 0:
        right, left = shift(parts[4], 1), shift(parts[-3], -1)
        right = shift(add(parts[3], right), 1)
        left = shift(add(parts[-2], left), -1)
        right = shift(add(parts[2], right), 1)
        left = shift(add(parts[-1], left), -1)
        right = shift(add(parts[1], right), 1)
    else:
        right, left = shift(parts[3], 1), shift(parts[4], -1)
        right = shift(add(parts[2], right), 1)
        left = shift(add(parts[-3], left), -1)
        right = shift(add(parts[1], right), 1)
        left = shift(add(parts[-2], left), -1)
        left = shift(add(parts[-1], left), -1)
    total = parts[0] + right.astype(jnp.float32) + left.astype(jnp.float32)
    return total.astype(jnp.bfloat16)


def local(queries, out_grads, latent, block_lists, block_home):
    ctx_count = lax.axis_size("ctx")
    head_count = lax.axis_size("head")
    me = lax.axis_index("head")
    groups, chosen = block_lists.shape
    tokens, heads, width = queries.shape
    value_width = out_grads.shape[2]
    group_rows = tokens // groups
    stored_blocks = latent.shape[0] // BLK
    entries = groups * chosen
    share = BLK // head_count
    subs = head_count // QUARTERS
    rows = group_rows * heads

    slot_of, requests, entry_of = plan(block_lists, block_home, ctx_count, stored_blocks)
    requests_in = lax.all_to_all(requests, "ctx", split_axis=0, concat_axis=0, tiled=True)

    stored = latent.reshape(stored_blocks, QUARTERS, subs, share, width)
    mine = lax.dynamic_index_in_dim(stored, me % QUARTERS, 1, keepdims=False)
    query_rows = queries.reshape(groups, rows, width)
    grad_rows = out_grads.reshape(groups, rows, value_width)
    requests_in, mine, query_rows = lax.optimization_barrier((requests_in, mine, query_rows))

    arrived = lax.all_to_all(
        take(requests_in, mine), "ctx", split_axis=0, concat_axis=0, tiled=True
    )
    part = chosen * BLK // QUARTERS
    own = pick(slot_of, arrived, groups).reshape(groups, part, width)

    right0, right1 = shift(own[0], 1), shift(own[1], 1)
    left1, left0 = shift(own[1], -1), shift(own[0], -1)
    far0, far1 = shift(right0, 1), shift(left1, -1)

    key_parts = [left0, right0, far0, left1, right1, far1]
    me_ref = me.astype(jnp.int32).reshape(1)
    query_cols, *parts = group_grads(me_ref, own, key_parts, query_rows, grad_rows)
    sums = []
    for group in range(groups):
        by_offset = {}
        for at in range(4):
            for which in range(2):
                by_offset[OFFSETS[at][which]] = parts[at * 2 + which][group]
        sums.append(ring_scatter(by_offset, group))
    query_grads = query_cols.reshape(groups, width, group_rows, heads)
    query_grads = query_grads.transpose(0, 2, 3, 1).reshape(tokens, heads, width)

    summed = jnp.concatenate(sums, axis=0).reshape(entries, share, width)
    returned = lax.all_to_all(
        take(entry_of, summed), "ctx", split_axis=0, concat_axis=0, tiled=True
    )
    total = gather_sum(requests_in, returned, stored_blocks)

    minus1, minus2 = shift(total, 1), shift(total, 2)
    plus1, plus2 = shift(total, -1), shift(total, -2)
    minus3, plus3, minus4 = shift(minus2, 1), shift(plus2, -1), shift(minus2, 2)
    pieces = jnp.stack([total, plus1, plus2, plus3, minus4, minus3, minus2, minus1])
    pieces = jnp.roll(pieces, me, axis=0)
    pieces = pieces.reshape(subs, QUARTERS, stored_blocks, share, width)
    latent_grads = pieces.transpose(2, 1, 0, 3, 4).reshape(stored_blocks * BLK, width)
    return query_grads, latent_grads.astype(jnp.float32)


def solution(mesh):
    in_specs = (P("ctx", "head", None), P("ctx", "head", None), P("ctx", None), P("ctx", None), P())
    out_specs = (P("ctx", "head", None), P("ctx", None))
    return jax.shard_map(local, mesh=mesh, in_specs=in_specs, out_specs=out_specs, check_vma=False)
```

```python
import functools

import jax
import jax.numpy as jnp
from jax import lax
from jax.experimental import pallas as pl
from jax.experimental.pallas import tpu as pltpu
from jax.sharding import PartitionSpec as P

BLK = 64
CAPACITY = 2
QUARTERS = 4
LOG2E = 1.4426950408889634
softmax_scale = 192.0 ** (-0.5)
VMEM_LIMIT = 56 * 1024 * 1024
ROWS_BY_ROWS = (((1,), (1,)), ((), ()))
COLS_BY_COLS = (((0,), (0,)), ((), ()))


def smem():
    return pl.BlockSpec(memory_space=pltpu.SMEM)


def vmem():
    return pl.BlockSpec(memory_space=pltpu.VMEM)


def plan_kernel(stored_blocks, lists_ref, home_ref, slot_ref, request_ref, entry_ref):
    groups, chosen = lists_ref.shape
    owners = request_ref.shape[0]
    for owner in range(owners):
        for copy in range(CAPACITY):
            request_ref[owner, 0, copy] = -1
            entry_ref[owner * CAPACITY + copy] = 0
    for group in range(groups):
        for at in range(chosen):
            entry = group * chosen + at
            stored = home_ref[lists_ref[group, at]]
            owner = stored // stored_blocks
            copy = jnp.where(request_ref[owner, 0, 0] >= 0, 1, 0)
            slot = owner * CAPACITY + copy
            slot_ref[entry] = slot
            request_ref[owner, 0, copy] = stored % stored_blocks
            entry_ref[slot] = entry


def plan(block_lists, block_home, ctx_count, stored_blocks):
    entries = block_lists.shape[0] * block_lists.shape[1]
    return pl.pallas_call(
        functools.partial(plan_kernel, stored_blocks),
        out_shape=(
            jax.ShapeDtypeStruct((entries,), jnp.int32),
            jax.ShapeDtypeStruct((ctx_count, 1, CAPACITY), jnp.int32),
            jax.ShapeDtypeStruct((ctx_count * CAPACITY,), jnp.int32),
        ),
        in_specs=[smem(), smem()],
        out_specs=(smem(), smem(), smem()),
        name="plan",
    )(block_lists, block_home)


def read_index(index_ref, at):
    if len(index_ref.shape) == 3:
        return index_ref[at // CAPACITY, 0, at % CAPACITY]
    return index_ref[at]


def take_kernel(index_ref, rows_ref, out_ref):
    for at in range(out_ref.shape[0]):
        out_ref[at] = rows_ref[jnp.maximum(read_index(index_ref, at), 0)]


def take(index, rows):
    return pl.pallas_call(
        take_kernel,
        out_shape=jax.ShapeDtypeStruct((index.size,) + rows.shape[1:], rows.dtype),
        in_specs=[smem(), vmem()],
        out_specs=vmem(),
        name="take",
    )(index, rows)


def pick_kernel(index_ref, rows_ref, both_ref, *group_refs):
    groups, subs, chosen = both_ref.shape[:3]
    for group in range(groups):
        for at in range(chosen):
            slot = index_ref[group * chosen + at]
            for sub in range(subs):
                row = rows_ref[slot, sub]
                both_ref[group, sub, at] = row
                group_refs[group][sub, at] = row


def pick(index, rows, groups):
    chosen = index.shape[0] // groups
    shape = (rows.shape[1], chosen) + rows.shape[2:]
    one = jax.ShapeDtypeStruct(shape, rows.dtype)
    return pl.pallas_call(
        pick_kernel,
        out_shape=[jax.ShapeDtypeStruct((groups,) + shape, rows.dtype)] + [one] * groups,
        in_specs=[smem(), vmem()],
        out_specs=[vmem()] * (groups + 1),
        name="pick",
    )(index, rows)


def sum_take_kernel(index_ref, *refs):
    term_refs, out_ref, total = refs[:-2], refs[-2], refs[-1]
    value = term_refs[0][...].astype(jnp.float32)
    for term in term_refs[1:]:
        value = value + term[...].astype(jnp.float32)
    total[...] = value.astype(total.dtype)
    for at in range(out_ref.shape[0]):
        out_ref[at] = total[index_ref[at]]


def sum_take(index, terms):
    kind = jnp.bfloat16
    return pl.pallas_call(
        sum_take_kernel,
        out_shape=jax.ShapeDtypeStruct((index.shape[0],) + terms[0].shape[1:], kind),
        in_specs=[smem()] + [vmem()] * len(terms),
        out_specs=vmem(),
        scratch_shapes=[pltpu.VMEM(terms[0].shape, kind)],
        name="sum_take",
    )(index, *terms)


def gather_sum_kernel(index_ref, rows_ref, out_ref, total):
    total[...] = jnp.zeros_like(total)
    stored = out_ref.shape[0]
    for at in range(rows_ref.shape[0]):
        index = read_index(index_ref, at)
        index = jnp.where(index < 0, stored, index)
        total[index] += rows_ref[at].astype(jnp.float32)
    out_ref[...] = total[:stored].astype(out_ref.dtype)


def gather_sum(index, rows, stored):
    return pl.pallas_call(
        gather_sum_kernel,
        out_shape=jax.ShapeDtypeStruct((stored,) + rows.shape[1:], jnp.bfloat16),
        in_specs=[smem(), vmem()],
        out_specs=vmem(),
        scratch_shapes=[pltpu.VMEM((stored + 1,) + rows.shape[1:], jnp.float32)],
        name="gather_sum",
    )(index, rows)


OFFSETS = ((0, 4), (1, -3), (-1, 3), (2, -2))


def group_kernel(value_width, me_ref, *refs):
    near_refs, far_refs = refs[:3], refs[3:5]
    query_ref, grad_ref = refs[5:7]
    query_out = refs[7]
    part_refs = refs[8:17]
    keys, sums = refs[17:]
    step = pl.program_id(0)
    part = near_refs[0].shape[0]

    for at in range(3):
        keys[at * part : (at + 1) * part, :] = near_refs[at][...]
    for group in range(2):

        @pl.when(step == group)
        def _():
            keys[3 * part :, :] = far_refs[group][...]

    scores = lax.dot_general(
        keys[...], query_ref[...], ROWS_BY_ROWS, preferred_element_type=jnp.float32
    )
    factor = softmax_scale * LOG2E
    top = jnp.max(scores, axis=0, keepdims=True) * factor
    raised = jnp.exp2(scores * factor - top)
    weights = raised * (1.0 / jnp.sum(raised, axis=0, keepdims=True))
    half = weights.astype(jnp.bfloat16)
    weight_grad = lax.dot_general(
        keys[:, :value_width], grad_ref[...], ROWS_BY_ROWS, preferred_element_type=jnp.float32
    )
    delta = jnp.sum(half.astype(jnp.float32) * weight_grad, axis=0, keepdims=True)
    score_half = (weights * (weight_grad - delta)).astype(jnp.bfloat16)
    from_scores = (
        jnp.dot(score_half, query_ref[...], preferred_element_type=jnp.float32) * softmax_scale
    )
    from_values = jnp.dot(half, grad_ref[...], preferred_element_type=jnp.float32)
    sums[:, :value_width] = from_scores[:, :value_width] + from_values
    sums[:, value_width:] = from_scores[:, value_width:]
    query_out[...] = (
        lax.dot_general(
            keys[...], score_half, COLS_BY_COLS, preferred_element_type=jnp.float32
        )
        * softmax_scale
    ).astype(jnp.bfloat16)

    me = me_ref[0]
    half_part = part // 2
    for at in range(4):
        sub = ((me + OFFSETS[at][0] + 8) % 8) // 4
        for which in range(2):
            use = sub if which == 0 else 1 - sub
            start = pl.multiple_of(at * part + use * half_part, half_part)
            value = sums[pl.ds(start, half_part), :]
            if OFFSETS[at][which] != 4:
                out = part_refs[at * 2 + which]
                out[...] = value.astype(out.dtype)
                continue
            for group in range(2):

                @pl.when(step == group)
                def _():
                    out = part_refs[1 + 7 * group]
                    out[...] = value.astype(out.dtype)


def group_grads(me, near, far, query_rows, grad_rows):
    groups, part, width = near[0].shape
    rows, value_width = grad_rows.shape[1:]
    key_count = QUARTERS * part
    by_group = lambda *shape: pl.BlockSpec((None,) + shape, lambda i: (i, 0, 0))
    whole = lambda *shape: pl.BlockSpec(shape, lambda i: (0, 0))
    out_shape = [jax.ShapeDtypeStruct((groups, width, rows), jnp.bfloat16)]
    out_specs = [by_group(width, rows)]
    for at in range(9):
        kind = jnp.float32 if at == 0 else jnp.bfloat16
        if at in (1, 8):
            out_shape.append(jax.ShapeDtypeStruct((part // 2, width), kind))
            out_specs.append(whole(part // 2, width))
        else:
            out_shape.append(jax.ShapeDtypeStruct((groups, part // 2, width), kind))
            out_specs.append(by_group(part // 2, width))
    flops = 2 * groups * rows * key_count * (3 * width + 2 * value_width)
    return pl.pallas_call(
        functools.partial(group_kernel, value_width),
        grid=(groups,),
        in_specs=[smem()]
        + [by_group(part, width)] * 3
        + [whole(part, width)] * 2
        + [by_group(rows, width), by_group(rows, value_width)],
        out_specs=out_specs,
        out_shape=out_shape,
        scratch_shapes=[
            pltpu.VMEM((key_count, width), jnp.bfloat16),
            pltpu.VMEM((key_count, width), jnp.float32),
        ],
        compiler_params=pltpu.CompilerParams(vmem_limit_bytes=VMEM_LIMIT),
        cost_estimate=pl.CostEstimate(
            flops=flops, bytes_accessed=15_000_000, transcendentals=groups * rows * key_count
        ),
        name="group_grads",
    )(me, *near, *far, query_rows, grad_rows)


def shift(x, by):
    count = lax.axis_size("head")
    return lax.ppermute(x, "head", [(i, (i + by) % count) for i in range(count)])


def add(*terms):
    return sum(term.astype(jnp.float32) for term in terms).astype(jnp.bfloat16)


def scatter_terms(outs):
    plus, minus = {}, {}
    own, far0, plus[1], minus[3], minus[1], plus[3], plus[2], minus[2], far1 = outs
    from_left, from_right = shift(plus[3], 1), shift(minus[3], -1)
    far_left, far_right = shift(far0, 2), shift(far1, -2)
    near_left, near_right = shift(plus[1], 1), shift(minus[1], -1)
    far_left = jnp.stack([far_left, jnp.zeros_like(far_left)])
    far_right = jnp.stack([jnp.zeros_like(far_right), far_right])
    two_left = shift(add(plus[2], from_left, far_left), 2)
    two_right = shift(add(minus[2], from_right, far_right), -2)
    return own, near_left, near_right, two_left, two_right


def local(queries, out_grads, latent, block_lists, block_home):
    ctx_count = lax.axis_size("ctx")
    head_count = lax.axis_size("head")
    me = lax.axis_index("head")
    groups, chosen = block_lists.shape
    tokens, heads, width = queries.shape
    value_width = out_grads.shape[2]
    group_rows = tokens // groups
    stored_blocks = latent.shape[0] // BLK
    entries = groups * chosen
    share = BLK // head_count
    subs = head_count // QUARTERS
    rows = group_rows * heads

    slot_of, requests, entry_of = plan(block_lists, block_home, ctx_count, stored_blocks)
    requests_in = lax.all_to_all(requests, "ctx", split_axis=0, concat_axis=0, tiled=True)

    stored = latent.reshape(stored_blocks, QUARTERS, subs, share, width)
    mine = lax.dynamic_index_in_dim(stored, me % QUARTERS, 1, keepdims=False)
    query_rows = queries.reshape(groups, rows, width)
    grad_rows = out_grads.reshape(groups, rows, value_width)
    requests_in, mine, query_rows = lax.optimization_barrier((requests_in, mine, query_rows))

    arrived = lax.all_to_all(
        take(requests_in, mine), "ctx", split_axis=0, concat_axis=0, tiled=True
    )
    part = chosen * BLK // QUARTERS
    own, own0, own1 = pick(slot_of, arrived, groups)
    own = own.reshape(groups, part, width)
    own0, own1 = own0.reshape(part, width), own1.reshape(part, width)

    near = [own, shift(own, -1), shift(own, 1)]
    far = [shift(own0, 2), shift(own1, -2)]
    me_ref = me.astype(jnp.int32).reshape(1)
    query_cols, *outs = group_grads(me_ref, near, far, query_rows, grad_rows)
    terms = [x.reshape(entries, share, width) for x in scatter_terms(outs)]
    query_grads = query_cols.reshape(groups, width, group_rows, heads)
    query_grads = query_grads.transpose(0, 2, 3, 1).reshape(tokens, heads, width)

    returned = lax.all_to_all(
        sum_take(entry_of, terms), "ctx", split_axis=0, concat_axis=0, tiled=True
    )
    total = gather_sum(requests_in, returned, stored_blocks)

    minus1, minus2 = shift(total, 1), shift(total, 2)
    plus1, plus2 = shift(total, -1), shift(total, -2)
    minus3, plus3, minus4 = shift(minus2, 1), shift(plus2, -1), shift(minus2, 2)
    pieces = jnp.stack([total, plus1, plus2, plus3, minus4, minus3, minus2, minus1])
    pieces = jnp.roll(pieces, me, axis=0)
    pieces = pieces.reshape(subs, QUARTERS, stored_blocks, share, width)
    latent_grads = pieces.transpose(2, 1, 0, 3, 4).reshape(stored_blocks * BLK, width)
    return query_grads, latent_grads.astype(jnp.float32)


def solution(mesh):
    in_specs = (P("ctx", "head", None), P("ctx", "head", None), P("ctx", None), P("ctx", None), P())
    out_specs = (P("ctx", "head", None), P("ctx", None))
    return jax.shard_map(local, mesh=mesh, in_specs=in_specs, out_specs=out_specs, check_vma=False)
```

```python
import functools

import jax
import jax.numpy as jnp
from jax import lax
from jax.experimental import pallas as pl
from jax.experimental.pallas import tpu as pltpu
from jax.sharding import PartitionSpec as P

BLK = 64
CAPACITY = 2
LOG2E = 1.4426950408889634
softmax_scale = 192.0 ** (-0.5)
VMEM_LIMIT = 56 * 1024 * 1024
ROWS_BY_ROWS = (((1,), (1,)), ((), ()))
COLS_BY_COLS = (((0,), (0,)), ((), ()))
OFFSETS = (0, 1, -1, 2, -2, 3, -3, 4)


def smem():
    return pl.BlockSpec(memory_space=pltpu.SMEM)


def vmem():
    return pl.BlockSpec(memory_space=pltpu.VMEM)


def one_hot(hit):
    return jnp.where(hit, 1.0, 0.0).astype(jnp.bfloat16)


def plan_kernel(stored_blocks, lists_ref, home_ref, entry_ref, count):
    groups, chosen = lists_ref.shape
    for owner in range(count.shape[0]):
        count[owner] = 0
    for slot in range(entry_ref.shape[0]):
        entry_ref[slot] = 0
    for group in range(groups):
        for at in range(chosen):
            owner = home_ref[lists_ref[group, at]] // stored_blocks
            earlier = count[owner]
            entry_ref[owner * CAPACITY + earlier] = group * chosen + at
            count[owner] = earlier + 1


def plan(block_lists, block_home, ctx_count, stored_blocks):
    return pl.pallas_call(
        functools.partial(plan_kernel, stored_blocks),
        out_shape=jax.ShapeDtypeStruct((ctx_count * CAPACITY,), jnp.int32),
        in_specs=[smem(), smem()],
        out_specs=smem(),
        scratch_shapes=[pltpu.SMEM((ctx_count,), jnp.int32)],
        name="plan",
    )(block_lists, block_home)


def spread_kernel(pair, lists_ref, home_ref, latent_ref, out_ref):
    width, tokens = latent_ref.shape
    stored = tokens // BLK
    span = stored * pair
    row = lax.broadcasted_iota(jnp.int32, (tokens, tokens), 0)
    col = lax.broadcasted_iota(jnp.int32, (tokens, tokens), 1)
    source = (row % span) // pair * BLK + row // span * pair + row % pair
    moved = lax.dot_general(
        one_hot(col == source),
        latent_ref[...],
        ROWS_BY_ROWS,
        preferred_element_type=jnp.float32,
    )
    out_ref[:, :width] = moved.astype(out_ref.dtype)
    free = out_ref.shape[1] - width
    entry = lax.broadcasted_iota(jnp.int32, (span, free), 0) // pair
    entry = entry + stored * lax.broadcasted_iota(jnp.int32, (span, free), 1)
    groups, chosen = lists_ref.shape
    value = jnp.zeros((span, free), jnp.float32)
    for group in range(groups):
        for at in range(chosen):
            position = home_ref[lists_ref[group, at]].astype(jnp.float32)
            value = jnp.where(entry == group * chosen + at, position, value)
    value = value.astype(out_ref.dtype)
    for start in range(0, tokens, span):
        out_ref[start : start + span, width:] = value


def spread(block_lists, block_home, latent_cols, pair):
    width, tokens = latent_cols.shape
    return pl.pallas_call(
        functools.partial(spread_kernel, pair),
        out_shape=jax.ShapeDtypeStruct((tokens, 640), latent_cols.dtype),
        in_specs=[smem(), smem(), vmem()],
        out_specs=vmem(),
        compiler_params=pltpu.CompilerParams(vmem_limit_bytes=VMEM_LIMIT),
        name="spread",
    )(block_lists, block_home, latent_cols)


def choose_kernel(pair, held_ref, out_ref):
    targets, steps, span, width = out_ref.shape
    count = held_ref.shape[0]
    rows = held_ref[:, :width]
    lists = held_ref[:, width:].astype(jnp.float32)
    parity = lax.broadcasted_iota(jnp.int32, (count, 1), 0) % pair
    col = lax.broadcasted_iota(jnp.int32, (count, count), 1).astype(jnp.float32)
    for step in range(steps):
        source = lists[:, step : step + 1] * pair + parity.astype(jnp.float32)
        chosen = jnp.dot(one_hot(col == source), rows, preferred_element_type=jnp.float32)
        out_ref[:, step] = chosen.astype(out_ref.dtype).reshape(targets, span, width)


def choose(held, width, targets, entries, pair):
    span = held.shape[0] // targets
    steps = entries * pair // span
    return pl.pallas_call(
        functools.partial(choose_kernel, pair),
        out_shape=jax.ShapeDtypeStruct((targets, steps, span, width), held.dtype),
        in_specs=[vmem()],
        out_specs=vmem(),
        compiler_params=pltpu.CompilerParams(vmem_limit_bytes=VMEM_LIMIT),
        name="choose",
    )(held)


def place_kernel(pair, index_ref, *refs):
    term_refs, out_ref, total, picks = refs[:-3], refs[-3], refs[-2], refs[-1]
    half = len(term_refs) // 2
    rows = term_refs[0].shape[0]
    share = out_ref.shape[1]
    spread_over = rows * pair // share
    for group in range(2):
        terms = term_refs[group * half : (group + 1) * half]
        value = terms[0][...].astype(jnp.float32)
        for term in terms[1:]:
            value = value + term[...].astype(jnp.float32)
        total[group * rows : (group + 1) * rows, :] = value.astype(total.dtype)
    row = lax.broadcasted_iota(jnp.int32, (share, 2 * rows), 0)
    col = lax.broadcasted_iota(jnp.int32, (share, 2 * rows), 1)
    lead = col - (row // pair * spread_over + row % pair)
    chosen = spread_over // pair
    for slot in range(out_ref.shape[0]):
        entry = index_ref[slot]
        start = entry // chosen * rows + entry % chosen * pair
        picks[slot * share : (slot + 1) * share, :] = jnp.where(lead == start, 1.0, 0.0)
    placed = jnp.dot(
        picks[...].astype(jnp.bfloat16), total[...], preferred_element_type=jnp.float32
    )
    out_ref[...] = placed.astype(out_ref.dtype).reshape(out_ref.shape)


def place(index, by_group, share, pair):
    terms = [term for group in by_group for term in group]
    rows, width = terms[0].shape
    slots = index.shape[0]
    return pl.pallas_call(
        functools.partial(place_kernel, pair),
        out_shape=jax.ShapeDtypeStruct((slots, share, width), jnp.bfloat16),
        in_specs=[smem()] + [vmem()] * len(terms),
        out_specs=vmem(),
        scratch_shapes=[
            pltpu.VMEM((2 * rows, width), jnp.bfloat16),
            pltpu.VMEM((slots * share, 2 * rows), jnp.float32),
        ],
        name="place",
    )(index, *terms)


def gather_sum_kernel(index_ref, rows_ref, out_ref, total):
    total[...] = jnp.zeros_like(total)
    stored = out_ref.shape[0]
    for at in range(rows_ref.shape[0]):
        index = index_ref[at]
        index = jnp.where(index < 0, stored, index)
        total[index] += rows_ref[at].astype(jnp.float32)
    out_ref[...] = total[:stored].astype(out_ref.dtype)


def gather_sum(index, rows, stored):
    return pl.pallas_call(
        gather_sum_kernel,
        out_shape=jax.ShapeDtypeStruct((stored,) + rows.shape[1:], jnp.bfloat16),
        in_specs=[smem(), vmem()],
        out_specs=vmem(),
        scratch_shapes=[pltpu.VMEM((stored + 1,) + rows.shape[1:], jnp.float32)],
        name="gather_sum",
    )(index, rows)


def group_kernel(me_ref, key_ref, query_ref, grad_ref, query_out, *refs):
    part_refs, sums = refs[:-1], refs[-1]
    step = pl.program_id(0)
    width = query_ref.shape[1]
    value_width = grad_ref.shape[1]
    keys = key_ref[...].reshape(sums.shape)

    scores = lax.dot_general(
        keys, query_ref[...], ROWS_BY_ROWS, preferred_element_type=jnp.float32
    )
    factor = softmax_scale * LOG2E
    top = jnp.max(scores, axis=0, keepdims=True) * factor
    raised = jnp.exp2(scores * factor - top)
    weights = raised * (1.0 / jnp.sum(raised, axis=0, keepdims=True))
    half = weights.astype(jnp.bfloat16)
    weight_grad = lax.dot_general(
        keys[:, :value_width], grad_ref[...], ROWS_BY_ROWS, preferred_element_type=jnp.float32
    )
    delta = jnp.sum(half.astype(jnp.float32) * weight_grad, axis=0, keepdims=True)
    score_half = (weights * (weight_grad - delta)).astype(jnp.bfloat16)
    from_scores = (
        jnp.dot(score_half, query_ref[...], preferred_element_type=jnp.float32) * softmax_scale
    )
    from_values = jnp.dot(half, grad_ref[...], preferred_element_type=jnp.float32)
    sums[:, :value_width] = from_scores[:, :value_width] + from_values
    sums[:, value_width:] = from_scores[:, value_width:]
    query_out[...] = (
        lax.dot_general(keys, score_half, COLS_BY_COLS, preferred_element_type=jnp.float32)
        * softmax_scale
    ).astype(jnp.bfloat16)

    me = me_ref[0]
    count = len(OFFSETS)
    part = sums.shape[0] // count
    for group in range(2):

        @pl.when(step == group)
        def _():
            for at, offset in enumerate(OFFSETS):
                start = pl.multiple_of((me + offset + count) % count * part, part)
                out = part_refs[group * count + at]
                out[...] = sums[pl.ds(start, part), :].astype(out.dtype)


def group_grads(me, keys, query_rows, grad_rows):
    sources, groups, span, width = keys.shape
    rows, value_width = grad_rows.shape[1:]
    key_count = sources * span
    part = key_count // len(OFFSETS)
    by_group = lambda *shape: pl.BlockSpec((None,) + shape, lambda i: (i, 0, 0))
    out_shape = [jax.ShapeDtypeStruct((groups, width, rows), jnp.bfloat16)]
    out_specs = [by_group(width, rows)]
    for _ in range(groups):
        for offset in OFFSETS:
            kind = jnp.float32 if offset == 0 else jnp.bfloat16
            out_shape.append(jax.ShapeDtypeStruct((part, width), kind))
            out_specs.append(pl.BlockSpec((part, width), lambda i: (0, 0)))
    flops = 2 * groups * rows * key_count * (3 * width + 2 * value_width)
    return pl.pallas_call(
        group_kernel,
        grid=(groups,),
        in_specs=[
            smem(),
            pl.BlockSpec((sources, None, span, width), lambda i: (0, i, 0, 0)),
            by_group(rows, width),
            by_group(rows, value_width),
        ],
        out_specs=out_specs,
        out_shape=out_shape,
        scratch_shapes=[pltpu.VMEM((key_count, width), jnp.float32)],
        compiler_params=pltpu.CompilerParams(vmem_limit_bytes=VMEM_LIMIT),
        cost_estimate=pl.CostEstimate(
            flops=flops, bytes_accessed=15_000_000, transcendentals=groups * rows * key_count
        ),
        name="group_grads",
    )(me, keys, query_rows, grad_rows)


def shift(x, by):
    count = lax.axis_size("head")
    return lax.ppermute(x, "head", [(i, (i + by) % count) for i in range(count)])


def add(a, b):
    return (a.astype(jnp.float32) + b.astype(jnp.float32)).astype(jnp.bfloat16)


def ring_scatter(parts, group):
    if group == 0:
        right, left = shift(parts[4], 1), shift(parts[-3], -1)
        right = shift(add(parts[3], right), 1)
        left = shift(add(parts[-2], left), -1)
        right = shift(add(parts[2], right), 1)
        left = shift(add(parts[-1], left), -1)
        right = shift(add(parts[1], right), 1)
    else:
        right, left = shift(parts[3], 1), shift(parts[4], -1)
        right = shift(add(parts[2], right), 1)
        left = shift(add(parts[-3], left), -1)
        right = shift(add(parts[1], right), 1)
        left = shift(add(parts[-2], left), -1)
        left = shift(add(parts[-1], left), -1)
    return parts[0], right, left


def requested(lists, me, stored_blocks):
    entry = lax.broadcasted_iota(jnp.int32, lists.shape, 1)
    code = entry * stored_blocks + lists % stored_blocks
    hit = lists // stored_blocks == me
    first = jnp.min(jnp.where(hit, code, 1 << 20), axis=1)
    last = jnp.max(jnp.where(hit, code, -1), axis=1)
    one = jnp.where(last >= 0, first % stored_blocks, -1)
    two = jnp.where(last > first, last % stored_blocks, -1)
    return jnp.stack([one, two], axis=1).reshape(-1)


def local(queries, out_grads, latent, block_lists, block_home):
    ctx_count = lax.axis_size("ctx")
    head_count = lax.axis_size("head")
    me = lax.axis_index("head")
    groups, chosen = block_lists.shape
    tokens, heads, width = queries.shape
    value_width = out_grads.shape[2]
    group_rows = tokens // groups
    stored_blocks = latent.shape[0] // BLK
    entries = groups * chosen
    share = BLK // head_count
    pair = BLK // ctx_count
    span = stored_blocks * pair
    rows = group_rows * heads

    spread_rows = spread(block_lists, block_home, latent.T, pair)
    held = lax.all_to_all(
        spread_rows.reshape(ctx_count, span, 640), "ctx", split_axis=0, concat_axis=0, tiled=True
    )
    query_rows = queries.reshape(groups, rows, width)
    grad_rows = out_grads.reshape(groups, rows, value_width)
    entry_of = plan(block_lists, block_home, ctx_count, stored_blocks)
    held, query_rows, entry_of = lax.optimization_barrier((held, query_rows, entry_of))

    outgoing = choose(held.reshape(ctx_count * span, 640), width, ctx_count, entries, pair)
    outgoing = outgoing.reshape(ctx_count, groups, chosen * pair, width)
    keys = lax.all_to_all(outgoing, "ctx", split_axis=0, concat_axis=0, tiled=True)

    lists = held[:, ::pair, width : width + entries * pair // span].astype(jnp.int32)
    lists = lists.transpose(0, 2, 1).reshape(ctx_count, entries)
    requests_in = requested(lists, lax.axis_index("ctx"), stored_blocks)

    me_ref = me.astype(jnp.int32).reshape(1)
    query_cols, *parts = group_grads(me_ref, keys, query_rows, grad_rows)
    by_group = []
    for group in range(groups):
        terms = parts[group * len(OFFSETS) : (group + 1) * len(OFFSETS)]
        by_group.append(ring_scatter(dict(zip(OFFSETS, terms)), group))
    query_grads = query_cols.reshape(groups, width, group_rows, heads)
    query_grads = query_grads.transpose(0, 2, 3, 1).reshape(tokens, heads, width)

    returned = lax.all_to_all(
        place(entry_of, by_group, share, pair), "ctx", split_axis=0, concat_axis=0, tiled=True
    )
    total = gather_sum(requests_in, returned, stored_blocks)

    minus1, minus2 = shift(total, 1), shift(total, 2)
    plus1, plus2 = shift(total, -1), shift(total, -2)
    minus3, plus3, minus4 = shift(minus2, 1), shift(plus2, -1), shift(minus2, 2)
    pieces = jnp.stack([total, plus1, plus2, plus3, minus4, minus3, minus2, minus1])
    pieces = jnp.roll(pieces, me, axis=0)
    latent_grads = pieces.transpose(1, 0, 2, 3).reshape(stored_blocks * BLK, width)
    return query_grads, latent_grads.astype(jnp.float32)


def solution(mesh):
    in_specs = (P("ctx", "head", None), P("ctx", "head", None), P("ctx", None), P("ctx", None), P())
    out_specs = (P("ctx", "head", None), P("ctx", None))
    return jax.shard_map(local, mesh=mesh, in_specs=in_specs, out_specs=out_specs, check_vma=False)
```

```python
import functools

import jax
import jax.numpy as jnp
from jax import lax
from jax.experimental import pallas as pl
from jax.experimental.pallas import tpu as pltpu
from jax.sharding import PartitionSpec as P

BLK = 64
CAPACITY = 2
LOG2E = 1.4426950408889634
softmax_scale = 192.0 ** (-0.5)
GROUP_LIMITS = (56 * 1024 * 1024, 56 * 1024 * 1024)
LARGE_LIMIT = 56 * 1024 * 1024
SMALL_LIMIT = 16 * 1024 * 1024
ROWS_BY_ROWS = (((1,), (1,)), ((), ()))
COLS_BY_COLS = (((0,), (0,)), ((), ()))
OFFSETS = (0, 1, -1, 2, -2, 3, -3, 4)


def smem():
    return pl.BlockSpec(memory_space=pltpu.SMEM)


def vmem():
    return pl.BlockSpec(memory_space=pltpu.VMEM)


def one_hot(hit):
    return jnp.where(hit, 1.0, 0.0).astype(jnp.bfloat16)


def plan_kernel(stored_blocks, lists_ref, home_ref, entry_ref, count):
    groups, chosen = lists_ref.shape
    for owner in range(count.shape[0]):
        count[owner] = 0
    for slot in range(entry_ref.shape[0]):
        entry_ref[slot] = 0
    for group in range(groups):
        for at in range(chosen):
            owner = home_ref[lists_ref[group, at]] // stored_blocks
            earlier = count[owner]
            entry_ref[owner * CAPACITY + earlier] = group * chosen + at
            count[owner] = earlier + 1


def plan(block_lists, block_home, ctx_count, stored_blocks):
    return pl.pallas_call(
        functools.partial(plan_kernel, stored_blocks),
        out_shape=jax.ShapeDtypeStruct((ctx_count * CAPACITY,), jnp.int32),
        in_specs=[smem(), smem()],
        out_specs=smem(),
        scratch_shapes=[pltpu.SMEM((ctx_count,), jnp.int32)],
        name="plan",
    )(block_lists, block_home)


def spread_kernel(pair, lists_ref, home_ref, latent_ref, out_ref):
    width, tokens = latent_ref.shape
    stored = tokens // BLK
    span = stored * pair
    row = lax.broadcasted_iota(jnp.int32, (tokens, tokens), 0)
    col = lax.broadcasted_iota(jnp.int32, (tokens, tokens), 1)
    source = (row % span) // pair * BLK + row // span * pair + row % pair
    moved = lax.dot_general(
        one_hot(col == source),
        latent_ref[...],
        ROWS_BY_ROWS,
        preferred_element_type=jnp.float32,
    )
    out_ref[:, :width] = moved.astype(out_ref.dtype)
    free = out_ref.shape[1] - width
    entry = lax.broadcasted_iota(jnp.int32, (span, free), 0) // pair
    entry = entry + stored * lax.broadcasted_iota(jnp.int32, (span, free), 1)
    groups, chosen = lists_ref.shape
    value = jnp.zeros((span, free), jnp.float32)
    for group in range(groups):
        for at in range(chosen):
            position = home_ref[lists_ref[group, at]].astype(jnp.float32)
            value = jnp.where(entry == group * chosen + at, position, value)
    value = value.astype(out_ref.dtype)
    for start in range(0, tokens, span):
        out_ref[start : start + span, width:] = value


def spread(block_lists, block_home, latent_cols, pair):
    width, tokens = latent_cols.shape
    return pl.pallas_call(
        functools.partial(spread_kernel, pair),
        out_shape=jax.ShapeDtypeStruct((tokens, 640), latent_cols.dtype),
        in_specs=[smem(), smem(), vmem()],
        out_specs=vmem(),
        compiler_params=pltpu.CompilerParams(vmem_limit_bytes=LARGE_LIMIT),
        name="spread",
    )(block_lists, block_home, latent_cols)


def choose_kernel(pair, me_ref, held_ref, half_ref, whole_ref):
    targets, span, width = half_ref.shape
    count = held_ref.shape[0]
    rows = held_ref[:, :width]
    lists = held_ref[:, width:].astype(jnp.float32)
    parity = lax.broadcasted_iota(jnp.int32, (count, 1), 0) % pair
    col = lax.broadcasted_iota(jnp.int32, (count, count), 1).astype(jnp.float32)
    odd = me_ref[0] % 2
    mine = jnp.where(odd == 0, lists[:, 0:1], lists[:, 1:2])
    for at, positions in enumerate((mine, lists[:, 2:3], lists[:, 3:4])):
        source = positions * pair + parity.astype(jnp.float32)
        chosen = jnp.dot(one_hot(col == source), rows, preferred_element_type=jnp.float32)
        chosen = chosen.astype(half_ref.dtype).reshape(targets, span, width)
        if at == 0:
            half_ref[...] = chosen
        else:
            whole_ref[:, (at - 1) * span : at * span] = chosen


def choose(me, held, width, targets, pair):
    span = held.shape[0] // targets
    return pl.pallas_call(
        functools.partial(choose_kernel, pair),
        out_shape=[
            jax.ShapeDtypeStruct((targets, span, width), held.dtype),
            jax.ShapeDtypeStruct((targets, 2 * span, width), held.dtype),
        ],
        in_specs=[smem(), vmem()],
        out_specs=[vmem(), vmem()],
        compiler_params=pltpu.CompilerParams(vmem_limit_bytes=SMALL_LIMIT),
        name="choose",
    )(me, held)


def place_kernel(pair, index_ref, *refs):
    term_refs, out_ref, total, picks = refs[:-3], refs[-3], refs[-2], refs[-1]
    half = len(term_refs) // 2
    rows = term_refs[0].shape[0]
    share = out_ref.shape[1]
    spread_over = rows * pair // share
    for group in range(2):
        terms = term_refs[group * half : (group + 1) * half]
        value = terms[0][...].astype(jnp.float32)
        for term in terms[1:]:
            value = value + term[...].astype(jnp.float32)
        total[group * rows : (group + 1) * rows, :] = value.astype(total.dtype)
    row = lax.broadcasted_iota(jnp.int32, (share, 2 * rows), 0)
    col = lax.broadcasted_iota(jnp.int32, (share, 2 * rows), 1)
    chosen = spread_over // pair
    lead0 = col - (row // pair * (spread_over // 2) + row % pair)
    lead1 = col - (row // pair * spread_over + row % pair)
    for slot in range(out_ref.shape[0]):
        entry = index_ref[slot]
        within = entry % (chosen // 2) * pair
        start0 = entry // (chosen // 2) * (rows // 2) + within
        start1 = rows + entry % chosen * pair
        away = jnp.where(entry < chosen, lead0 - start0, lead1 - start1)
        picks[slot * share : (slot + 1) * share, :] = jnp.where(away == 0, 1.0, 0.0)
    placed = jnp.dot(
        picks[...].astype(jnp.bfloat16), total[...], preferred_element_type=jnp.float32
    )
    out_ref[...] = placed.astype(out_ref.dtype).reshape(out_ref.shape)


def place(index, by_group, share, pair):
    terms = [term for group in by_group for term in group]
    rows, width = terms[0].shape
    slots = index.shape[0]
    return pl.pallas_call(
        functools.partial(place_kernel, pair),
        out_shape=jax.ShapeDtypeStruct((slots, share, width), jnp.bfloat16),
        in_specs=[smem()] + [vmem()] * len(terms),
        out_specs=vmem(),
        scratch_shapes=[
            pltpu.VMEM((2 * rows, width), jnp.bfloat16),
            pltpu.VMEM((slots * share, 2 * rows), jnp.float32),
        ],
        compiler_params=pltpu.CompilerParams(vmem_limit_bytes=SMALL_LIMIT),
        name="place",
    )(index, *terms)


def gather_sum_kernel(index_ref, rows_ref, out_ref, total):
    total[...] = jnp.zeros_like(total)
    stored = out_ref.shape[0]
    for at in range(rows_ref.shape[0]):
        index = index_ref[at]
        index = jnp.where(index < 0, stored, index)
        total[index] += rows_ref[at].astype(jnp.float32)
    out_ref[...] = total[:stored].astype(out_ref.dtype)


def gather_sum(index, rows, stored):
    return pl.pallas_call(
        gather_sum_kernel,
        out_shape=jax.ShapeDtypeStruct((stored,) + rows.shape[1:], jnp.bfloat16),
        in_specs=[smem(), vmem()],
        out_specs=vmem(),
        scratch_shapes=[pltpu.VMEM((stored + 1,) + rows.shape[1:], jnp.float32)],
        compiler_params=pltpu.CompilerParams(vmem_limit_bytes=SMALL_LIMIT),
        name="gather_sum",
    )(index, rows)


def group_kernel(key_count, me_ref, *refs):
    key_refs, (query_ref, grad_ref, query_out) = refs[:key_count], refs[key_count : key_count + 3]
    part_refs, sums = refs[key_count + 3 : -1], refs[-1]
    width = query_ref.shape[1]
    value_width = grad_ref.shape[1]
    keys = [ref[...].reshape(-1, width) for ref in key_refs]
    keys = keys[0] if key_count == 1 else jnp.concatenate(keys, axis=0)

    scores = lax.dot_general(
        keys, query_ref[...], ROWS_BY_ROWS, preferred_element_type=jnp.float32
    )
    factor = softmax_scale * LOG2E
    top = jnp.max(scores, axis=0, keepdims=True) * factor
    raised = jnp.exp2(scores * factor - top)
    weights = raised * (1.0 / jnp.sum(raised, axis=0, keepdims=True))
    half = weights.astype(jnp.bfloat16)
    weight_grad = lax.dot_general(
        keys[:, :value_width], grad_ref[...], ROWS_BY_ROWS, preferred_element_type=jnp.float32
    )
    delta = jnp.sum(half.astype(jnp.float32) * weight_grad, axis=0, keepdims=True)
    score_half = (weights * (weight_grad - delta)).astype(jnp.bfloat16)
    from_scores = (
        jnp.dot(score_half, query_ref[...], preferred_element_type=jnp.float32) * softmax_scale
    )
    from_values = jnp.dot(half, grad_ref[...], preferred_element_type=jnp.float32)
    sums[:, :value_width] = from_scores[:, :value_width] + from_values
    sums[:, value_width:] = from_scores[:, value_width:]
    query_out[...] = (
        lax.dot_general(keys, score_half, COLS_BY_COLS, preferred_element_type=jnp.float32)
        * softmax_scale
    ).astype(jnp.bfloat16)

    me = me_ref[0]
    count = len(OFFSETS)
    part = sums.shape[0] // count
    half_part = part // 2
    for out, offset in zip(part_refs, OFFSETS):
        place = (me + offset + count) % count
        if key_count == 1:
            start = pl.multiple_of(place * part, part)
            out[...] = sums[pl.ds(start, part), :].astype(out.dtype)
            continue
        for which in range(2):
            begin = (which + me) % 2 * (count * half_part) + place * half_part
            begin = pl.multiple_of(begin, half_part)
            value = sums[pl.ds(begin, half_part), :]
            out[which * half_part : (which + 1) * half_part, :] = value.astype(out.dtype)


def group_grads(group, me, keys, query_rows, grad_rows):
    key_count = sum(x.shape[0] * x.shape[1] for x in keys)
    width = keys[0].shape[2]
    rows, value_width = grad_rows.shape[1:]
    part = key_count // len(OFFSETS)
    by_group = lambda *shape: pl.BlockSpec((None,) + shape, lambda i: (group, 0, 0))
    whole = lambda *shape: pl.BlockSpec(shape, lambda i: (0,) * len(shape))
    out_shape = [jax.ShapeDtypeStruct((width, rows), jnp.bfloat16)]
    for offset in OFFSETS:
        kind = jnp.float32 if offset == 0 else jnp.bfloat16
        out_shape.append(jax.ShapeDtypeStruct((part, width), kind))
    flops = 2 * rows * key_count * (3 * width + 2 * value_width)
    return pl.pallas_call(
        functools.partial(group_kernel, len(keys)),
        grid=(1,),
        in_specs=[smem()]
        + [whole(*x.shape) for x in keys]
        + [by_group(rows, width), by_group(rows, value_width)],
        out_specs=[whole(*shape.shape) for shape in out_shape],
        out_shape=out_shape,
        scratch_shapes=[pltpu.VMEM((key_count, width), jnp.float32)],
        compiler_params=pltpu.CompilerParams(vmem_limit_bytes=GROUP_LIMITS[group]),
        cost_estimate=pl.CostEstimate(
            flops=flops, bytes_accessed=8_000_000, transcendentals=rows * key_count
        ),
        name="group_grads",
    )(me, *keys, query_rows, grad_rows)


def shift(x, by):
    count = lax.axis_size("head")
    return lax.ppermute(x, "head", [(i, (i + by) % count) for i in range(count)])


def add(a, b):
    return (a.astype(jnp.float32) + b.astype(jnp.float32)).astype(jnp.bfloat16)


def ring_start(parts):
    return shift(parts[4], 1), shift(parts[-3], -1)


def ring_end(parts, right, left):
    right, left = shift(add(parts[3], right), 1), shift(add(parts[-2], left), -1)
    right, left = shift(add(parts[2], right), 1), shift(add(parts[-1], left), -1)
    return parts[0], shift(add(parts[1], right), 1), left


def ring_whole(parts):
    right, left = shift(parts[3], 1), shift(parts[4], -1)
    right, left = shift(add(parts[2], right), 1), shift(add(parts[-3], left), -1)
    right, left = shift(add(parts[1], right), 1), shift(add(parts[-2], left), -1)
    return parts[0], right, shift(add(parts[-1], left), -1)


def requested(lists, me, stored_blocks):
    entry = lax.broadcasted_iota(jnp.int32, lists.shape, 1)
    code = entry * stored_blocks + lists % stored_blocks
    hit = lists // stored_blocks == me
    first = jnp.min(jnp.where(hit, code, 1 << 20), axis=1)
    last = jnp.max(jnp.where(hit, code, -1), axis=1)
    one = jnp.where(last >= 0, first % stored_blocks, -1)
    two = jnp.where(last > first, last % stored_blocks, -1)
    return jnp.stack([one, two], axis=1).reshape(-1)


def local(queries, out_grads, latent, block_lists, block_home):
    ctx_count = lax.axis_size("ctx")
    head_count = lax.axis_size("head")
    me = lax.axis_index("head")
    groups, chosen = block_lists.shape
    tokens, heads, width = queries.shape
    value_width = out_grads.shape[2]
    group_rows = tokens // groups
    stored_blocks = latent.shape[0] // BLK
    entries = groups * chosen
    share = BLK // head_count
    pair = BLK // ctx_count
    span = stored_blocks * pair
    rows = group_rows * heads

    spread_rows = spread(block_lists, block_home, latent.T, pair)
    held = lax.all_to_all(
        spread_rows.reshape(ctx_count, span, 640), "ctx", split_axis=0, concat_axis=0, tiled=True
    )
    query_rows = queries.reshape(groups, rows, width)
    grad_rows = out_grads.reshape(groups, rows, value_width)
    entry_of = plan(block_lists, block_home, ctx_count, stored_blocks)
    held, query_rows, entry_of = lax.optimization_barrier((held, query_rows, entry_of))

    me_ref = me.astype(jnp.int32).reshape(1)
    outgoing = choose(me_ref, held.reshape(ctx_count * span, 640), width, ctx_count, pair)
    own, keys1 = [
        lax.all_to_all(x, "ctx", split_axis=0, concat_axis=0, tiled=True) for x in outgoing
    ]
    middle = ctx_count // 2
    keys0 = [own, shift(own[:middle], 1), shift(own[middle:], -1)]

    lists = held[:, ::pair, width : width + entries * pair // span].astype(jnp.int32)
    lists = lists.transpose(0, 2, 1).reshape(ctx_count, entries)
    requests_in = requested(lists, lax.axis_index("ctx"), stored_blocks)

    query_cols0, *parts0 = group_grads(0, me_ref, keys0, query_rows, grad_rows)
    parts0 = dict(zip(OFFSETS, parts0))
    right, left = ring_start(parts0)
    query_cols1, *parts1 = group_grads(1, me_ref, [keys1], query_rows, grad_rows)
    parts1[0], right, left = lax.optimization_barrier((parts1[0], right, left))
    by_group = [ring_end(parts0, right, left), ring_whole(dict(zip(OFFSETS, parts1)))]
    query_cols = jnp.stack([query_cols0, query_cols1])
    query_grads = query_cols.reshape(groups, width, group_rows, heads)
    query_grads = query_grads.transpose(0, 2, 3, 1).reshape(tokens, heads, width)

    returned = lax.all_to_all(
        place(entry_of, by_group, share, pair), "ctx", split_axis=0, concat_axis=0, tiled=True
    )
    total = gather_sum(requests_in, returned, stored_blocks)

    minus1, minus2 = shift(total, 1), shift(total, 2)
    plus1, plus2 = shift(total, -1), shift(total, -2)
    minus3, plus3, minus4 = shift(minus2, 1), shift(plus2, -1), shift(minus2, 2)
    pieces = jnp.stack([total, plus1, plus2, plus3, minus4, minus3, minus2, minus1])
    pieces = jnp.roll(pieces, me, axis=0)
    latent_grads = pieces.transpose(1, 0, 2, 3).reshape(stored_blocks * BLK, width)
    return query_grads, latent_grads.astype(jnp.float32)


def solution(mesh):
    in_specs = (P("ctx", "head", None), P("ctx", "head", None), P("ctx", None), P("ctx", None), P())
    out_specs = (P("ctx", "head", None), P("ctx", None))
    return jax.shard_map(local, mesh=mesh, in_specs=in_specs, out_specs=out_specs, check_vma=False)
```

```python
import functools

import jax
import jax.numpy as jnp
from jax import lax
from jax.experimental import pallas as pl
from jax.experimental.pallas import tpu as pltpu
from jax.sharding import PartitionSpec as P

BLK = 64
CAPACITY = 2
LOG2E = 1.4426950408889634
softmax_scale = 192.0 ** (-0.5)
LARGE_LIMIT = 56 * 1024 * 1024
SMALL_LIMIT = 16 * 1024 * 1024
ROWS_BY_ROWS = (((1,), (1,)), ((), ()))
COLS_BY_COLS = (((0,), (0,)), ((), ()))
OFFSETS = (0, 1, -1, 2, -2, 3, -3, 4)


def smem():
    return pl.BlockSpec(memory_space=pltpu.SMEM)


def vmem():
    return pl.BlockSpec(memory_space=pltpu.VMEM)


def one_hot(hit):
    return jnp.where(hit, 1.0, 0.0).astype(jnp.bfloat16)


def plan_kernel(stored_blocks, lists_ref, home_ref, entry_ref, count):
    groups, chosen = lists_ref.shape
    for owner in range(count.shape[0]):
        count[owner] = 0
    for slot in range(entry_ref.shape[0]):
        entry_ref[slot] = 0
    for group in range(groups):
        for at in range(chosen):
            owner = home_ref[lists_ref[group, at]] // stored_blocks
            earlier = count[owner]
            entry_ref[owner * CAPACITY + earlier] = group * chosen + at
            count[owner] = earlier + 1


def plan(block_lists, block_home, ctx_count, stored_blocks):
    return pl.pallas_call(
        functools.partial(plan_kernel, stored_blocks),
        out_shape=jax.ShapeDtypeStruct((ctx_count * CAPACITY,), jnp.int32),
        in_specs=[smem(), smem()],
        out_specs=smem(),
        scratch_shapes=[pltpu.SMEM((ctx_count,), jnp.int32)],
        name="plan",
    )(block_lists, block_home)


def spread_kernel(pair, lists_ref, home_ref, latent_ref, out_ref):
    width, tokens = latent_ref.shape
    stored = tokens // BLK
    span = stored * pair
    row = lax.broadcasted_iota(jnp.int32, (tokens, tokens), 0)
    col = lax.broadcasted_iota(jnp.int32, (tokens, tokens), 1)
    source = (row % span) // pair * BLK + row // span * pair + row % pair
    moved = lax.dot_general(
        one_hot(col == source),
        latent_ref[...],
        ROWS_BY_ROWS,
        preferred_element_type=jnp.float32,
    )
    out_ref[:, :width] = moved.astype(out_ref.dtype)
    free = out_ref.shape[1] - width
    entry = lax.broadcasted_iota(jnp.int32, (span, free), 0) // pair
    entry = entry + stored * lax.broadcasted_iota(jnp.int32, (span, free), 1)
    groups, chosen = lists_ref.shape
    value = jnp.zeros((span, free), jnp.float32)
    for group in range(groups):
        for at in range(chosen):
            position = home_ref[lists_ref[group, at]].astype(jnp.float32)
            value = jnp.where(entry == group * chosen + at, position, value)
    value = value.astype(out_ref.dtype)
    for start in range(0, tokens, span):
        out_ref[start : start + span, width:] = value


def spread(block_lists, block_home, latent_cols, pair):
    width, tokens = latent_cols.shape
    return pl.pallas_call(
        functools.partial(spread_kernel, pair),
        out_shape=jax.ShapeDtypeStruct((tokens, 640), latent_cols.dtype),
        in_specs=[smem(), smem(), vmem()],
        out_specs=vmem(),
        compiler_params=pltpu.CompilerParams(vmem_limit_bytes=LARGE_LIMIT),
        name="spread",
    )(block_lists, block_home, latent_cols)


def choose_kernel(pair, held_ref, *out_refs):
    targets, _, width = out_refs[0].shape
    count = held_ref.shape[0]
    span = count // targets
    steps = out_refs[0].shape[1] // span
    rows = held_ref[:, :width]
    lists = held_ref[:, width:].astype(jnp.float32)
    parity = lax.broadcasted_iota(jnp.int32, (count, 1), 0) % pair
    col = lax.broadcasted_iota(jnp.int32, (count, count), 1).astype(jnp.float32)
    for group, out_ref in enumerate(out_refs):
        for step in range(steps):
            at = group * steps + step
            source = lists[:, at : at + 1] * pair + parity.astype(jnp.float32)
            chosen = jnp.dot(one_hot(col == source), rows, preferred_element_type=jnp.float32)
            chosen = chosen.astype(out_ref.dtype).reshape(targets, span, width)
            out_ref[:, step * span : (step + 1) * span] = chosen


def choose(held, width, targets, groups, chosen, pair):
    one = jax.ShapeDtypeStruct((targets, chosen * pair, width), held.dtype)
    return pl.pallas_call(
        functools.partial(choose_kernel, pair),
        out_shape=[one] * groups,
        in_specs=[vmem()],
        out_specs=[vmem()] * groups,
        compiler_params=pltpu.CompilerParams(vmem_limit_bytes=SMALL_LIMIT),
        name="choose",
    )(held)


def place_kernel(pair, index_ref, *refs):
    term_refs, out_ref, total, picks = refs[:-3], refs[-3], refs[-2], refs[-1]
    half = len(term_refs) // 2
    rows = term_refs[0].shape[0]
    share = out_ref.shape[1]
    spread_over = rows * pair // share
    for group in range(2):
        terms = term_refs[group * half : (group + 1) * half]
        value = terms[0][...].astype(jnp.float32)
        for term in terms[1:]:
            value = value + term[...].astype(jnp.float32)
        total[group * rows : (group + 1) * rows, :] = value.astype(total.dtype)
    row = lax.broadcasted_iota(jnp.int32, (share, 2 * rows), 0)
    col = lax.broadcasted_iota(jnp.int32, (share, 2 * rows), 1)
    lead = col - (row // pair * spread_over + row % pair)
    chosen = spread_over // pair

    def one_slot(slot, carry):
        entry = index_ref[slot]
        start = entry // chosen * rows + entry % chosen * pair
        at = pl.multiple_of(slot * share, share)
        picks[pl.ds(at, share), :] = jnp.where(lead == start, 1.0, 0.0)
        return carry

    lax.fori_loop(0, out_ref.shape[0], one_slot, 0, unroll=4)
    placed = jnp.dot(
        picks[...].astype(jnp.bfloat16), total[...], preferred_element_type=jnp.float32
    )
    out_ref[...] = placed.astype(out_ref.dtype).reshape(out_ref.shape)


def place(index, by_group, share, pair):
    terms = [term for group in by_group for term in group]
    rows, width = terms[0].shape
    slots = index.shape[0]
    return pl.pallas_call(
        functools.partial(place_kernel, pair),
        out_shape=jax.ShapeDtypeStruct((slots, share, width), jnp.bfloat16),
        in_specs=[smem()] + [vmem()] * len(terms),
        out_specs=vmem(),
        scratch_shapes=[
            pltpu.VMEM((2 * rows, width), jnp.bfloat16),
            pltpu.VMEM((slots * share, 2 * rows), jnp.float32),
        ],
        compiler_params=pltpu.CompilerParams(vmem_limit_bytes=SMALL_LIMIT),
        name="place",
    )(index, *terms)


def gather_sum_kernel(index_ref, rows_ref, out_ref, total):
    total[...] = jnp.zeros_like(total)
    stored = out_ref.shape[0]

    def one_slot(at, carry):
        index = index_ref[at]
        index = jnp.where(index < 0, stored, index)
        total[index] += rows_ref[at].astype(jnp.float32)
        return carry

    lax.fori_loop(0, rows_ref.shape[0], one_slot, 0, unroll=4)
    out_ref[...] = total[:stored].astype(out_ref.dtype)


def gather_sum(index, rows, stored):
    return pl.pallas_call(
        gather_sum_kernel,
        out_shape=jax.ShapeDtypeStruct((stored,) + rows.shape[1:], jnp.bfloat16),
        in_specs=[smem(), vmem()],
        out_specs=vmem(),
        scratch_shapes=[pltpu.VMEM((stored + 1,) + rows.shape[1:], jnp.float32)],
        compiler_params=pltpu.CompilerParams(vmem_limit_bytes=SMALL_LIMIT),
        name="gather_sum",
    )(index, rows)


def each(count, total, do):
    if count == 1:
        do(slice(None))
        return
    size = total // count

    def one(at, carry):
        do(pl.ds(pl.multiple_of(at * size, size), size))
        return carry

    lax.fori_loop(0, count, one, 0)


def group_kernel(pieces, me_ref, key_ref, query_ref, grad_ref, query_out, *refs):
    part_refs, (sums, halves, score_halves) = refs[:-3], refs[-3:]
    rows, width = query_ref.shape
    value_width = grad_ref.shape[1]
    keys = key_ref[...].reshape(sums.shape)

    def weigh(cols):
        scores = lax.dot_general(
            keys, query_ref[cols, :], ROWS_BY_ROWS, preferred_element_type=jnp.float32
        )
        factor = softmax_scale * LOG2E
        top = jnp.max(scores, axis=0, keepdims=True) * factor
        raised = jnp.exp2(scores * factor - top)
        weights = raised * (1.0 / jnp.sum(raised, axis=0, keepdims=True))
        half = weights.astype(jnp.bfloat16)
        weight_grad = lax.dot_general(
            keys[:, :value_width],
            grad_ref[cols, :],
            ROWS_BY_ROWS,
            preferred_element_type=jnp.float32,
        )
        delta = jnp.sum(half.astype(jnp.float32) * weight_grad, axis=0, keepdims=True)
        halves[:, cols] = half
        score_halves[:, cols] = (weights * (weight_grad - delta)).astype(jnp.bfloat16)

    def key_sums(at):
        from_scores = (
            jnp.dot(score_halves[at, :], query_ref[...], preferred_element_type=jnp.float32)
            * softmax_scale
        )
        from_values = jnp.dot(halves[at, :], grad_ref[...], preferred_element_type=jnp.float32)
        sums[at, :value_width] = from_scores[:, :value_width] + from_values
        sums[at, value_width:] = from_scores[:, value_width:]

    def query_sums(cols):
        query_out[:, cols] = (
            lax.dot_general(
                keys, score_halves[:, cols], COLS_BY_COLS, preferred_element_type=jnp.float32
            )
            * softmax_scale
        ).astype(jnp.bfloat16)

    each(pieces, rows, weigh)
    each(pieces, sums.shape[0], key_sums)
    each(pieces, rows, query_sums)

    me = me_ref[0]
    count = len(OFFSETS)
    part = sums.shape[0] // count
    for out, offset in zip(part_refs, OFFSETS):
        start = pl.multiple_of((me + offset + count) % count * part, part)
        out[...] = sums[pl.ds(start, part), :].astype(out.dtype)


def group_grads(group, pieces, me, keys, query_rows, grad_rows):
    key_count = keys.shape[0] * keys.shape[1]
    width = keys.shape[2]
    rows, value_width = grad_rows.shape[1:]
    part = key_count // len(OFFSETS)
    by_group = lambda *shape: pl.BlockSpec((None,) + shape, lambda i: (group, 0, 0))
    whole = lambda *shape: pl.BlockSpec(shape, lambda i: (0,) * len(shape))
    out_shape = [jax.ShapeDtypeStruct((width, rows), jnp.bfloat16)]
    for offset in OFFSETS:
        kind = jnp.float32 if offset == 0 else jnp.bfloat16
        out_shape.append(jax.ShapeDtypeStruct((part, width), kind))
    flops = 2 * rows * key_count * (3 * width + 2 * value_width)
    return pl.pallas_call(
        functools.partial(group_kernel, pieces),
        grid=(1,),
        in_specs=[
            smem(),
            whole(*keys.shape),
            by_group(rows, width),
            by_group(rows, value_width),
        ],
        out_specs=[whole(*shape.shape) for shape in out_shape],
        out_shape=out_shape,
        scratch_shapes=[
            pltpu.VMEM((key_count, width), jnp.float32),
            pltpu.VMEM((key_count, rows), jnp.bfloat16),
            pltpu.VMEM((key_count, rows), jnp.bfloat16),
        ],
        compiler_params=pltpu.CompilerParams(vmem_limit_bytes=LARGE_LIMIT),
        cost_estimate=pl.CostEstimate(
            flops=flops, bytes_accessed=8_000_000, transcendentals=rows * key_count
        ),
        name="group_grads",
    )(me, keys, query_rows, grad_rows)


def shift(x, by):
    count = lax.axis_size("head")
    return lax.ppermute(x, "head", [(i, (i + by) % count) for i in range(count)])


def add(a, b):
    return (a.astype(jnp.float32) + b.astype(jnp.float32)).astype(jnp.bfloat16)


def ring_start(parts):
    return shift(parts[4], 1), shift(parts[-3], -1)


def ring_end(parts, right, left):
    right, left = shift(add(parts[3], right), 1), shift(add(parts[-2], left), -1)
    right, left = shift(add(parts[2], right), 1), shift(add(parts[-1], left), -1)
    return parts[0], shift(add(parts[1], right), 1), left


def ring_whole(parts):
    right, left = shift(parts[3], 1), shift(parts[4], -1)
    right, left = shift(add(parts[2], right), 1), shift(add(parts[-3], left), -1)
    right, left = shift(add(parts[1], right), 1), shift(add(parts[-2], left), -1)
    return parts[0], right, shift(add(parts[-1], left), -1)


def requested(lists, me, stored_blocks):
    entry = lax.broadcasted_iota(jnp.int32, lists.shape, 1)
    code = entry * stored_blocks + lists % stored_blocks
    hit = lists // stored_blocks == me
    first = jnp.min(jnp.where(hit, code, 1 << 20), axis=1)
    last = jnp.max(jnp.where(hit, code, -1), axis=1)
    one = jnp.where(last >= 0, first % stored_blocks, -1)
    two = jnp.where(last > first, last % stored_blocks, -1)
    return jnp.stack([one, two], axis=1).reshape(-1)


def local(queries, out_grads, latent, block_lists, block_home):
    ctx_count = lax.axis_size("ctx")
    head_count = lax.axis_size("head")
    me = lax.axis_index("head")
    groups, chosen = block_lists.shape
    tokens, heads, width = queries.shape
    value_width = out_grads.shape[2]
    group_rows = tokens // groups
    stored_blocks = latent.shape[0] // BLK
    entries = groups * chosen
    share = BLK // head_count
    pair = BLK // ctx_count
    span = stored_blocks * pair
    rows = group_rows * heads

    spread_rows = spread(block_lists, block_home, latent.T, pair)
    held = lax.all_to_all(
        spread_rows.reshape(ctx_count, span, 640), "ctx", split_axis=0, concat_axis=0, tiled=True
    )
    query_rows = queries.reshape(groups, rows, width)
    grad_rows = out_grads.reshape(groups, rows, value_width)
    entry_of = plan(block_lists, block_home, ctx_count, stored_blocks)
    held, query_rows, entry_of = lax.optimization_barrier((held, query_rows, entry_of))

    outgoing = choose(
        held.reshape(ctx_count * span, 640), width, ctx_count, groups, chosen, pair
    )
    keys0 = lax.all_to_all(outgoing[0], "ctx", split_axis=0, concat_axis=0, tiled=True)
    outgoing1, keys0 = lax.optimization_barrier((outgoing[1], keys0))
    keys1 = lax.all_to_all(outgoing1, "ctx", split_axis=0, concat_axis=0, tiled=True)

    lists = held[:, ::pair, width : width + entries * pair // span].astype(jnp.int32)
    lists = lists.transpose(0, 2, 1).reshape(ctx_count, entries)
    requests_in = requested(lists, lax.axis_index("ctx"), stored_blocks)

    me_ref = me.astype(jnp.int32).reshape(1)
    query_cols0, *parts0 = group_grads(0, 4, me_ref, keys0, query_rows, grad_rows)
    parts0 = dict(zip(OFFSETS, parts0))
    right, left = ring_start(parts0)
    query_cols1, *parts1 = group_grads(1, 1, me_ref, keys1, query_rows, grad_rows)
    parts1[0], right, left = lax.optimization_barrier((parts1[0], right, left))
    by_group = [ring_end(parts0, right, left), ring_whole(dict(zip(OFFSETS, parts1)))]
    query_cols = jnp.stack([query_cols0, query_cols1])
    query_grads = query_cols.reshape(groups, width, group_rows, heads)
    query_grads = query_grads.transpose(0, 2, 3, 1).reshape(tokens, heads, width)

    returned = lax.all_to_all(
        place(entry_of, by_group, share, pair), "ctx", split_axis=0, concat_axis=0, tiled=True
    )
    total = gather_sum(requests_in, returned, stored_blocks)

    minus1, minus2 = shift(total, 1), shift(total, 2)
    plus1, plus2 = shift(total, -1), shift(total, -2)
    minus3, plus3, minus4 = shift(minus2, 1), shift(plus2, -1), shift(minus2, 2)
    pieces = jnp.stack([total, plus1, plus2, plus3, minus4, minus3, minus2, minus1])
    pieces = jnp.roll(pieces, me, axis=0)
    latent_grads = pieces.transpose(1, 0, 2, 3).reshape(stored_blocks * BLK, width)
    return query_grads, latent_grads.astype(jnp.float32)


def solution(mesh):
    in_specs = (P("ctx", "head", None), P("ctx", "head", None), P("ctx", None), P("ctx", None), P())
    out_specs = (P("ctx", "head", None), P("ctx", None))
    return jax.shard_map(local, mesh=mesh, in_specs=in_specs, out_specs=out_specs, check_vma=False)
```

```python
import functools

import jax
import jax.numpy as jnp
from jax import lax
from jax.experimental import pallas as pl
from jax.experimental.pallas import tpu as pltpu
from jax.sharding import PartitionSpec as P

BLK = 64
CAPACITY = 2
LOG2E = 1.4426950408889634
softmax_scale = 192.0 ** (-0.5)
LARGE_LIMIT = 56 * 1024 * 1024
GROUP_LIMITS = (56 * 1024 * 1024, 50 * 1024 * 1024)
SMALL_LIMIT = 16 * 1024 * 1024
ROWS_BY_ROWS = (((1,), (1,)), ((), ()))
COLS_BY_COLS = (((0,), (0,)), ((), ()))
OFFSETS = (0, 1, -1, 2, -2, 3, -3, 4)


def smem():
    return pl.BlockSpec(memory_space=pltpu.SMEM)


def vmem():
    return pl.BlockSpec(memory_space=pltpu.VMEM)


def one_hot(hit):
    return jnp.where(hit, 1.0, 0.0).astype(jnp.bfloat16)


def plan_kernel(stored_blocks, lists_ref, home_ref, entry_ref, count):
    groups, chosen = lists_ref.shape
    for owner in range(count.shape[0]):
        count[owner] = 0
    for slot in range(entry_ref.shape[0]):
        entry_ref[slot] = 0
    for group in range(groups):
        for at in range(chosen):
            owner = home_ref[lists_ref[group, at]] // stored_blocks
            earlier = count[owner]
            entry_ref[owner * CAPACITY + earlier] = group * chosen + at
            count[owner] = earlier + 1


def plan(block_lists, block_home, ctx_count, stored_blocks):
    return pl.pallas_call(
        functools.partial(plan_kernel, stored_blocks),
        out_shape=jax.ShapeDtypeStruct((ctx_count * CAPACITY,), jnp.int32),
        in_specs=[smem(), smem()],
        out_specs=smem(),
        scratch_shapes=[pltpu.SMEM((ctx_count,), jnp.int32)],
        name="plan",
    )(block_lists, block_home)


def spread_kernel(pair, lists_ref, home_ref, latent_ref, out_ref):
    width, tokens = latent_ref.shape
    stored = tokens // BLK
    span = stored * pair
    row = lax.broadcasted_iota(jnp.int32, (tokens, 1), 0)
    col = lax.broadcasted_iota(jnp.int32, (tokens, tokens), 1)
    source = (row % span) // pair * BLK + row // span * pair + row % pair
    moved = lax.dot_general(
        one_hot(col == source),
        latent_ref[...],
        ROWS_BY_ROWS,
        preferred_element_type=jnp.float32,
    )
    out_ref[:, :width] = moved.astype(out_ref.dtype)
    free = out_ref.shape[1] - width
    entry = lax.broadcasted_iota(jnp.int32, (span, free), 0) // pair
    entry = entry + stored * lax.broadcasted_iota(jnp.int32, (span, free), 1)
    groups, chosen = lists_ref.shape
    value = jnp.zeros((span, free), jnp.float32)
    for group in range(groups):
        for at in range(chosen):
            position = home_ref[lists_ref[group, at]].astype(jnp.float32)
            value = jnp.where(entry == group * chosen + at, position, value)
    value = value.astype(out_ref.dtype)
    for start in range(0, tokens, span):
        out_ref[start : start + span, width:] = value


def spread(block_lists, block_home, latent_cols, pair):
    width, tokens = latent_cols.shape
    return pl.pallas_call(
        functools.partial(spread_kernel, pair),
        out_shape=jax.ShapeDtypeStruct((tokens, 640), latent_cols.dtype),
        in_specs=[smem(), smem(), vmem()],
        out_specs=vmem(),
        compiler_params=pltpu.CompilerParams(vmem_limit_bytes=LARGE_LIMIT),
        name="spread",
    )(block_lists, block_home, latent_cols)


def choose_kernel(first, pair, held_ref, out_ref):
    targets, total, width = out_ref.shape
    count = held_ref.shape[0]
    span = count // targets
    parity = lax.broadcasted_iota(jnp.int32, (count, 1), 0) % pair
    col = lax.broadcasted_iota(jnp.int32, (count, count), 1).astype(jnp.float32)
    for step in range(total // span):
        at = width + first + step
        positions = held_ref[:, at : at + 1].astype(jnp.float32)
        source = positions * pair + parity.astype(jnp.float32)
        chosen = jnp.dot(
            one_hot(col == source), held_ref[:, :width], preferred_element_type=jnp.float32
        )
        chosen = chosen.astype(out_ref.dtype).reshape(targets, span, width)
        out_ref[:, step * span : (step + 1) * span] = chosen


def choose(group, held, width, targets, chosen, pair):
    span = held.shape[0] // targets
    return pl.pallas_call(
        functools.partial(choose_kernel, group * chosen * pair // span, pair),
        out_shape=jax.ShapeDtypeStruct((targets, chosen * pair, width), held.dtype),
        in_specs=[vmem()],
        out_specs=vmem(),
        compiler_params=pltpu.CompilerParams(vmem_limit_bytes=(SMALL_LIMIT, LARGE_LIMIT)[group]),
        cost_estimate=pl.CostEstimate(
            flops=4 * held.shape[0] ** 2 * width, bytes_accessed=2_000_000, transcendentals=0
        ),
        name="choose",
    )(held)


def place_kernel(pair, index_ref, *refs):
    term_refs, out_ref, total, picks = refs[:-3], refs[-3], refs[-2], refs[-1]
    half = len(term_refs) // 2
    rows = term_refs[0].shape[0]
    share = out_ref.shape[1]
    spread_over = rows * pair // share
    for group in range(2):
        terms = term_refs[group * half : (group + 1) * half]
        value = terms[0][...].astype(jnp.float32)
        for term in terms[1:]:
            value = value + term[...].astype(jnp.float32)
        total[group * rows : (group + 1) * rows, :] = value.astype(total.dtype)
    row = lax.broadcasted_iota(jnp.int32, (share, 2 * rows), 0)
    col = lax.broadcasted_iota(jnp.int32, (share, 2 * rows), 1)
    lead = col - (row // pair * spread_over + row % pair)
    chosen = spread_over // pair

    def one_slot(slot, carry):
        entry = index_ref[slot]
        start = entry // chosen * rows + entry % chosen * pair
        at = pl.multiple_of(slot * share, share)
        picks[pl.ds(at, share), :] = jnp.where(lead == start, 1.0, 0.0)
        return carry

    lax.fori_loop(0, out_ref.shape[0], one_slot, 0, unroll=4)
    placed = jnp.dot(
        picks[...].astype(jnp.bfloat16), total[...], preferred_element_type=jnp.float32
    )
    out_ref[...] = placed.astype(out_ref.dtype).reshape(out_ref.shape)


def place(index, by_group, share, pair):
    terms = [term for group in by_group for term in group]
    rows, width = terms[0].shape
    slots = index.shape[0]
    return pl.pallas_call(
        functools.partial(place_kernel, pair),
        out_shape=jax.ShapeDtypeStruct((slots, share, width), jnp.bfloat16),
        in_specs=[smem()] + [vmem()] * len(terms),
        out_specs=vmem(),
        scratch_shapes=[
            pltpu.VMEM((2 * rows, width), jnp.bfloat16),
            pltpu.VMEM((slots * share, 2 * rows), jnp.float32),
        ],
        compiler_params=pltpu.CompilerParams(vmem_limit_bytes=SMALL_LIMIT),
        name="place",
    )(index, *terms)


def gather_sum_kernel(index_ref, rows_ref, out_ref, total):
    total[...] = jnp.zeros_like(total)
    stored = out_ref.shape[0]

    def one_slot(at, carry):
        index = index_ref[at]
        index = jnp.where(index < 0, stored, index)
        total[index] += rows_ref[at].astype(jnp.float32)
        return carry

    lax.fori_loop(0, rows_ref.shape[0], one_slot, 0, unroll=4)
    out_ref[...] = total[:stored].astype(out_ref.dtype)


def gather_sum(index, rows, stored):
    return pl.pallas_call(
        gather_sum_kernel,
        out_shape=jax.ShapeDtypeStruct((stored,) + rows.shape[1:], jnp.bfloat16),
        in_specs=[smem(), vmem()],
        out_specs=vmem(),
        scratch_shapes=[pltpu.VMEM((stored + 1,) + rows.shape[1:], jnp.float32)],
        compiler_params=pltpu.CompilerParams(vmem_limit_bytes=SMALL_LIMIT),
        name="gather_sum",
    )(index, rows)


def each(count, total, do):
    if count == 1:
        do(slice(None))
        return
    size = total // count

    def one(at, carry):
        do(pl.ds(pl.multiple_of(at * size, size), size))
        return carry

    lax.fori_loop(0, count, one, 0)


def group_kernel(pieces, me_ref, key_ref, query_ref, grad_ref, query_out, *refs):
    part_refs, (sums, halves, score_halves) = refs[:-3], refs[-3:]
    rows, width = query_ref.shape
    value_width = grad_ref.shape[1]
    keys = key_ref[...].reshape(sums.shape)

    def weigh(cols):
        scores = lax.dot_general(
            keys, query_ref[cols, :], ROWS_BY_ROWS, preferred_element_type=jnp.float32
        )
        factor = softmax_scale * LOG2E
        top = jnp.max(scores, axis=0, keepdims=True) * factor
        raised = jnp.exp2(scores * factor - top)
        weights = raised * (1.0 / jnp.sum(raised, axis=0, keepdims=True))
        half = weights.astype(jnp.bfloat16)
        weight_grad = lax.dot_general(
            keys[:, :value_width],
            grad_ref[cols, :],
            ROWS_BY_ROWS,
            preferred_element_type=jnp.float32,
        )
        delta = jnp.sum(half.astype(jnp.float32) * weight_grad, axis=0, keepdims=True)
        halves[:, cols] = half
        score_halves[:, cols] = (weights * (weight_grad - delta)).astype(jnp.bfloat16)

    def key_sums(at):
        from_scores = (
            jnp.dot(score_halves[at, :], query_ref[...], preferred_element_type=jnp.float32)
            * softmax_scale
        )
        from_values = jnp.dot(halves[at, :], grad_ref[...], preferred_element_type=jnp.float32)
        sums[at, :value_width] = from_scores[:, :value_width] + from_values
        sums[at, value_width:] = from_scores[:, value_width:]

    def query_sums(cols):
        query_out[:, cols] = (
            lax.dot_general(
                keys, score_halves[:, cols], COLS_BY_COLS, preferred_element_type=jnp.float32
            )
            * softmax_scale
        ).astype(jnp.bfloat16)

    each(pieces, rows, weigh)
    each(pieces, sums.shape[0], key_sums)
    each(pieces, rows, query_sums)

    me = me_ref[0]
    count = len(OFFSETS)
    part = sums.shape[0] // count
    for out, offset in zip(part_refs, OFFSETS):
        start = pl.multiple_of((me + offset + count) % count * part, part)
        out[...] = sums[pl.ds(start, part), :].astype(out.dtype)


def group_grads(group, pieces, me, keys, query_rows, grad_rows):
    key_count = keys.shape[0] * keys.shape[1]
    width = keys.shape[2]
    rows, value_width = grad_rows.shape[1:]
    part = key_count // len(OFFSETS)
    by_group = lambda *shape: pl.BlockSpec((None,) + shape, lambda i: (group, 0, 0))
    whole = lambda *shape: pl.BlockSpec(shape, lambda i: (0,) * len(shape))
    out_shape = [jax.ShapeDtypeStruct((width, rows), jnp.bfloat16)]
    for offset in OFFSETS:
        kind = jnp.float32 if offset == 0 else jnp.bfloat16
        out_shape.append(jax.ShapeDtypeStruct((part, width), kind))
    flops = 2 * rows * key_count * (3 * width + 2 * value_width)
    return pl.pallas_call(
        functools.partial(group_kernel, pieces),
        grid=(1,),
        in_specs=[
            smem(),
            whole(*keys.shape),
            by_group(rows, width),
            by_group(rows, value_width),
        ],
        out_specs=[whole(*shape.shape) for shape in out_shape],
        out_shape=out_shape,
        scratch_shapes=[
            pltpu.VMEM((key_count, width), jnp.float32),
            pltpu.VMEM((key_count, rows), jnp.bfloat16),
            pltpu.VMEM((key_count, rows), jnp.bfloat16),
        ],
        compiler_params=pltpu.CompilerParams(vmem_limit_bytes=GROUP_LIMITS[group]),
        cost_estimate=pl.CostEstimate(
            flops=flops, bytes_accessed=8_000_000, transcendentals=rows * key_count
        ),
        name="group_grads",
    )(me, keys, query_rows, grad_rows)


def shift(x, by):
    count = lax.axis_size("head")
    return lax.ppermute(x, "head", [(i, (i + by) % count) for i in range(count)])


def add(a, b):
    return (a.astype(jnp.float32) + b.astype(jnp.float32)).astype(jnp.bfloat16)


def ring_start(parts):
    return shift(parts[4], 1), shift(parts[-3], -1)


def ring_end(parts, right, left):
    right, left = shift(add(parts[3], right), 1), shift(add(parts[-2], left), -1)
    right, left = shift(add(parts[2], right), 1), shift(add(parts[-1], left), -1)
    return parts[0], shift(add(parts[1], right), 1), left


def ring_whole(parts):
    right, left = shift(parts[3], 1), shift(parts[4], -1)
    right, left = shift(add(parts[2], right), 1), shift(add(parts[-3], left), -1)
    right, left = shift(add(parts[1], right), 1), shift(add(parts[-2], left), -1)
    return parts[0], right, shift(add(parts[-1], left), -1)


def requested(lists, me, stored_blocks):
    entry = lax.broadcasted_iota(jnp.int32, lists.shape, 1)
    code = entry * stored_blocks + lists % stored_blocks
    hit = lists // stored_blocks == me
    first = jnp.min(jnp.where(hit, code, 1 << 20), axis=1)
    last = jnp.max(jnp.where(hit, code, -1), axis=1)
    one = jnp.where(last >= 0, first % stored_blocks, -1)
    two = jnp.where(last > first, last % stored_blocks, -1)
    return jnp.stack([one, two], axis=1).reshape(-1)


def local(queries, out_grads, latent, block_lists, block_home):
    ctx_count = lax.axis_size("ctx")
    head_count = lax.axis_size("head")
    me = lax.axis_index("head")
    groups, chosen = block_lists.shape
    tokens, heads, width = queries.shape
    value_width = out_grads.shape[2]
    group_rows = tokens // groups
    stored_blocks = latent.shape[0] // BLK
    entries = groups * chosen
    share = BLK // head_count
    pair = BLK // ctx_count
    span = stored_blocks * pair
    rows = group_rows * heads

    spread_rows = spread(block_lists, block_home, latent.T, pair)
    held = lax.all_to_all(
        spread_rows.reshape(ctx_count, span, 640), "ctx", split_axis=0, concat_axis=0, tiled=True
    )
    query_rows = queries.reshape(groups, rows, width)
    grad_rows = out_grads.reshape(groups, rows, value_width)
    entry_of = plan(block_lists, block_home, ctx_count, stored_blocks)
    held, query_rows, entry_of = lax.optimization_barrier((held, query_rows, entry_of))

    held_rows = held.reshape(ctx_count * span, 640)
    outgoing = [
        choose(group, held_rows, width, ctx_count, chosen, pair) for group in range(groups)
    ]
    keys0 = lax.all_to_all(outgoing[0], "ctx", split_axis=0, concat_axis=0, tiled=True)
    outgoing1, keys0 = lax.optimization_barrier((outgoing[1], keys0))
    keys1 = lax.all_to_all(outgoing1, "ctx", split_axis=0, concat_axis=0, tiled=True)

    lists = held[:, ::pair, width : width + entries * pair // span].astype(jnp.int32)
    lists = lists.transpose(0, 2, 1).reshape(ctx_count, entries)
    requests_in = requested(lists, lax.axis_index("ctx"), stored_blocks)

    me_ref = me.astype(jnp.int32).reshape(1)
    query_cols0, *parts0 = group_grads(0, 4, me_ref, keys0, query_rows, grad_rows)
    parts0 = dict(zip(OFFSETS, parts0))
    right, left = ring_start(parts0)
    query_cols1, *parts1 = group_grads(1, 1, me_ref, keys1, query_rows, grad_rows)
    parts1[0], right, left = lax.optimization_barrier((parts1[0], right, left))
    by_group = [ring_end(parts0, right, left), ring_whole(dict(zip(OFFSETS, parts1)))]
    query_cols = jnp.stack([query_cols0, query_cols1])
    query_grads = query_cols.reshape(groups, width, group_rows, heads)
    query_grads = query_grads.transpose(0, 2, 3, 1).reshape(tokens, heads, width)

    returned = lax.all_to_all(
        place(entry_of, by_group, share, pair), "ctx", split_axis=0, concat_axis=0, tiled=True
    )
    total = gather_sum(requests_in, returned, stored_blocks)

    minus1, minus2 = shift(total, 1), shift(total, 2)
    plus1, plus2 = shift(total, -1), shift(total, -2)
    minus3, plus3, minus4 = shift(minus2, 1), shift(plus2, -1), shift(minus2, 2)
    pieces = jnp.stack([total, plus1, plus2, plus3, minus4, minus3, minus2, minus1])
    pieces = jnp.roll(pieces, me, axis=0)
    latent_grads = pieces.transpose(1, 0, 2, 3).reshape(stored_blocks * BLK, width)
    return query_grads, latent_grads.astype(jnp.float32)


def solution(mesh):
    in_specs = (P("ctx", "head", None), P("ctx", "head", None), P("ctx", None), P("ctx", None), P())
    out_specs = (P("ctx", "head", None), P("ctx", None))
    return jax.shard_map(local, mesh=mesh, in_specs=in_specs, out_specs=out_specs, check_vma=False)
```
